512 devices in a mesh: gx: 128 (over x, z, y_lo, core), gy: 4 (over y_hi).
Axes of the slice: x: 4, y: 8 (y_hi: 4, y_lo: 2; y = y_hi * 2 + y_lo), z: 8, core: 2. Of those that a mesh axis runs over, the one named last changes fastest.
Arguments:
- gas_state: float32 [14, 1536, 1024], P(None, 'gx', 'gy'), may hold values from -2 to 8, as said below
- inflow: float32 [14, 1024], P(None, 'gy'), may hold values from -2 to 8, as said below
- slide_count: int32 [1], replicated, may hold values from 1 to 6
- cut_list: int32 [129], replicated, may hold values from 0 to 1536, as said below
- prefactor: float32 [8], replicated, may hold values from 4 to 40
- activation: float32 [8], replicated, may hold values from 1 to 4
- heat_release: float32 [8], replicated, may hold values from 2 to 8
Outputs:
- slabs: float32 [14, 1920, 1024], P(None, 'gx', 'gy')
The draws below stay inside these ranges and needn't reach their ends.
Inputs may be any that keep to these rules, and one draw needn't show every extreme that they name: `gas_state`: conserved variables of a gas with density between 0.5 and 2, pressure between 0.8 and 2, each velocity component between -0.6 and 0.6, and mass fractions summing to one. `inflow`: conserved variables of a gas with density between 0.5 and 2, pressure between 0.8 and 2, each velocity component between -0.6 and 0.6, and mass fractions summing to one. cut_list[0] = 0, cut_list[128] = 1536, increasing; every slab has 9 to 15 planes, exactly 15 on some device; cut_list[i] differs from i * 12 by at most 3.
All inputs are finite; a program needn't handle non-finite values.
Results may differ from the reference program's by a relative error of at most 0.00002.
Values sent between devices are 32-bit elements; how exact they have to be, the bound alone decides.
A program may use at most 64 MiB of HBM per device.

```python
import math
import jax
import jax.numpy as jnp
from jax import lax

NV = 14
NS = 9
NR = 8
PX = 12
NZ = 32
BAL = 3
CAP = 15
NX = 1536
NY = 32
N_GX = 128


def gas_mixture(key, tail, velocity):
    keys = jax.random.split(key, 3)
    density = jnp.exp(jax.random.uniform(keys[0], tail, jnp.float32, math.log(0.5), math.log(2.0)))
    pressure = jnp.exp(jax.random.uniform(keys[1], tail, jnp.float32, math.log(0.8), math.log(2.0)))
    weights = jax.random.uniform(keys[2], (NS,) + tail, jnp.float32, 0.2, 1.8)
    fractions = weights / jnp.sum(weights, axis=0)
    energy = pressure / 0.4 + 0.5 * density * jnp.sum(velocity * velocity, axis=0)
    return jnp.concatenate([density[None], density * velocity, energy[None], density * fractions], axis=0)


def draw_gas_state(key, part):
    key = jax.random.fold_in(key, 11)
    speed_key, rest_key = jax.random.split(key)
    tail = (NX, NY, NZ)
    velocity = jnp.clip(0.3 * jax.random.normal(speed_key, (3,) + tail, jnp.float32), -0.6, 0.6)
    return gas_mixture(rest_key, tail, velocity).reshape(NV, NX, NY * NZ)


def draw_inflow(key, part):
    key = jax.random.fold_in(key, 12)
    speed_key, rest_key = jax.random.split(key)
    tail = (NY, NZ)
    velocity = jnp.clip(0.3 * jax.random.normal(speed_key, (3,) + tail, jnp.float32), -0.6, 0.6)
    return gas_mixture(rest_key, tail, velocity).reshape(NV, NY * NZ)


def draw_cut_list(key, part):
    key = jax.random.fold_in(key, 13)
    spread_key, chosen_key, sign_key = jax.random.split(key, 3)
    pair_count = N_GX // 2
    spread = jax.random.randint(spread_key, (pair_count,), 0, BAL + 1)
    chosen = jax.random.randint(chosen_key, (), 0, pair_count)
    spread = jnp.where(jnp.arange(pair_count) == chosen, BAL, spread)
    signs = jax.random.randint(sign_key, (pair_count,), 0, 2) * 2 - 1
    slab_sizes = jnp.stack([PX + signs * spread, PX - signs * spread], axis=1).reshape(-1)
    return jnp.concatenate([jnp.zeros((1,), jnp.int32), jnp.cumsum(slab_sizes).astype(jnp.int32)])


def setup_inputs(seed: int = 0) -> dict:
    splits = jax.random.split(jax.random.key(seed), 8)
    gas_state = draw_gas_state(jax.random.fold_in(splits[7], 71), 0)
    inflow = draw_inflow(jax.random.fold_in(splits[7], 71), 0)
    slide_count = jax.random.randint(splits[2], (1,), 1, PX // 2 + 1).astype(jnp.int32)
    cut_list = draw_cut_list(jax.random.fold_in(splits[7], 71), 0)
    prefactor = jnp.clip(jnp.exp(jax.random.uniform(splits[4], (NR,), jnp.float32, math.log(4.0), math.log(40.0))), 4.0, 40.0)
    activation = jnp.clip(jax.random.uniform(splits[5], (NR,), jnp.float32, 1.0, 4.0), 1.0, 4.0)
    heat_release = jnp.clip(jax.random.uniform(splits[6], (NR,), jnp.float32, 2.0, 8.0), 2.0, 8.0)
    return dict(gas_state=gas_state, inflow=inflow, slide_count=slide_count, cut_list=cut_list, prefactor=prefactor, activation=activation, heat_release=heat_release)


GAS_GAMMA = 1.4
TIME_STEP = 0.025

def to_primitive(conserved):
    density = conserved[0]
    velocity = conserved[1:4] / density
    kinetic = 0.5 * density * lax.optimization_barrier(jnp.sum(velocity * velocity, axis=0))
    pressure = (GAS_GAMMA - 1.0) * (conserved[4] - kinetic)
    fractions = conserved[5:] / density
    return jnp.concatenate([density[None], velocity, pressure[None], fractions], axis=0)

def reconstruct(values, axis, extent):
    stencil = [lax.slice_in_dim(values, offset, offset + extent + 1, axis=axis) for offset in range(6)]
    upwind_low = (2.0 * stencil[0] - 13.0 * stencil[1] + 47.0 * stencil[2] + 27.0 * stencil[3] - 3.0 * stencil[4]) / 60.0
    upwind_high = (-3.0 * stencil[1] + 27.0 * stencil[2] + 47.0 * stencil[3] - 13.0 * stencil[4] + 2.0 * stencil[5]) / 60.0
    return (upwind_low, upwind_high)

def physical(values, direction):
    density = values[0]
    velocity = values[1:4]
    pressure = values[4]
    fractions = values[5:]
    normal = velocity[direction]
    energy = pressure / (GAS_GAMMA - 1.0) + 0.5 * density * lax.optimization_barrier(jnp.sum(velocity * velocity, axis=0))
    conserved = jnp.concatenate([density[None], density * velocity, energy[None], density * fractions], axis=0)
    fluxes = conserved * normal
    fluxes = fluxes.at[1 + direction].add(pressure)
    fluxes = fluxes.at[4].add(pressure * normal)
    wave_speed = jnp.abs(normal) + jnp.sqrt(GAS_GAMMA * pressure / density)
    return (conserved, fluxes, wave_speed)

def divergence(padded, axis, direction):
    extent = padded.shape[axis] - 6
    upwind_low, upwind_high = reconstruct(to_primitive(padded), axis, extent)
    cons_low, flux_low, speed_low = physical(upwind_low, direction)
    cons_high, flux_high, speed_high = physical(upwind_high, direction)
    fluxes = 0.5 * (flux_low + flux_high) - 0.5 * jnp.maximum(speed_low, speed_high) * (cons_high - cons_low)
    return lax.slice_in_dim(fluxes, 1, extent + 1, axis=axis) - lax.slice_in_dim(fluxes, 0, extent, axis=axis)

def chemistry(primitive, prefactor, activation, heat_release):
    density = primitive[0]
    pressure = primitive[4]
    fractions = primitive[5:]
    reaction_rates = prefactor.reshape(-1, 1, 1, 1) * density * fractions[:-1] * jnp.exp(-activation.reshape(-1, 1, 1, 1) * density / pressure)
    species = jnp.concatenate([-reaction_rates[:1], reaction_rates[:-1] - reaction_rates[1:], reaction_rates[-1:]], axis=0)
    release = lax.optimization_barrier(jnp.sum(heat_release.reshape(-1, 1, 1, 1) * reaction_rates, axis=0))
    no_source = jnp.zeros((4,) + density.shape, density.dtype)
    return jnp.concatenate([no_source, release[None], species], axis=0)

def tendency(x_padded, y_padded, interior, prefactor, activation, heat_release):
    z_padded = jnp.concatenate([interior[..., -3:], interior, interior[..., :3]], axis=3)
    total = divergence(x_padded, 1, 0) + divergence(y_padded, 2, 1) + divergence(z_padded, 3, 2)
    return chemistry(to_primitive(interior), prefactor, activation, heat_release) - total

def mirror(edge_rows):
    wall_sign = jnp.where(jnp.arange(edge_rows.shape[0]) == 2, -1.0, 1.0).astype(edge_rows.dtype).reshape(-1, 1, 1, 1)
    return jnp.flip(edge_rows, axis=2) * wall_sign

def global_tendency(field, inflow, prefactor, activation, heat_release):
    ghost_low = jnp.repeat(field[:, :1], 3, axis=1)
    ghost_high = jnp.repeat(inflow[:, None], 3, axis=1)
    padded = jnp.concatenate([ghost_low, field, ghost_high], axis=1)

    def block(block_start):
        x_padded = lax.dynamic_slice_in_dim(padded, block_start, PX + 6, 1)
        interior = x_padded[:, 3:-3]
        y_padded = jnp.concatenate([mirror(interior[:, :, :3]), interior, mirror(interior[:, :, -3:])], axis=2)
        return tendency(x_padded, y_padded, interior, prefactor, activation, heat_release)
    block_starts = jnp.arange(N_GX, dtype=jnp.int32) * PX
    blocks = lax.map(block, block_starts)
    return jnp.moveaxis(blocks, 0, 1).reshape(NV, NX, NY, NZ)

def reference(gas_state, inflow, slide_count, cut_list, prefactor, activation, heat_release):
    field = gas_state.reshape(NV, NX, NY, NZ)
    fresh_gas = inflow.reshape(NV, NY, NZ)
    plane_ids = jnp.arange(NX, dtype=jnp.int32) + slide_count[0]
    shifted = jnp.take(field, jnp.minimum(plane_ids, NX - 1), axis=1)
    window = jnp.where((plane_ids < NX)[None, :, None, None], shifted, fresh_gas[:, None])
    segment_one = window + TIME_STEP * global_tendency(window, fresh_gas, prefactor, activation, heat_release)
    segment_two = 0.75 * window + 0.25 * (segment_one + TIME_STEP * global_tendency(segment_one, fresh_gas, prefactor, activation, heat_release))
    slot_ids = jnp.arange(CAP, dtype=jnp.int32)
    source_plane = cut_list[:-1][:, None] + slot_ids[None, :]
    is_valid = (source_plane < cut_list[1:][:, None]).reshape(-1)
    source_plane = jnp.minimum(source_plane, NX - 1).reshape(-1)
    laid_out = jnp.take(segment_two, source_plane, axis=1)
    laid_out = jnp.where(is_valid[None, :, None, None], laid_out, jnp.zeros_like(laid_out))
    return laid_out.reshape(NV, N_GX * CAP, NY * NZ)
```

```python
import functools

import jax
import jax.numpy as jnp
from jax import lax
from jax.experimental import pallas as pl
from jax.experimental.pallas import tpu as pltpu
from jax.sharding import PartitionSpec as P

MESH = pl.DeviceIdType.MESH
NV = 14
NR = 8
PX = 12
CAP = 15
NZ = 32
GAS_GAMMA = 1.4
TIME_STEP = 0.025

OWN = 8 * NV
NEXT = OWN + PX * NV
Y_OWN = 4 * NV
Y_NEXT = Y_OWN + PX * NV
V_OWN = 4 * NV
G_OWN = 12 * NV

W_ROWS = 560
Y_ROWS = 424
V_ROWS = 56 + 24 * NV
G_ROWS = 352

LOW = (2.0, -13.0, 47.0, 27.0, -3.0, 0.0)
HIGH = (0.0, -3.0, 27.0, 47.0, -13.0, 2.0)


def stencil_pair(q):
    d = [c / 60.0 for c in (2.0, 13.0, 47.0, 27.0, 3.0)]
    low = (d[0] * q[0] - d[1] * q[1]) + (d[2] * q[2] + d[3] * q[3]) - d[4] * q[4]
    high = (d[3] * q[2] - d[4] * q[1]) + (d[2] * q[3] - d[1] * q[4]) + d[0] * q[5]
    return low, high


def wave_speed(normal, pressure, density):
    scaled = GAS_GAMMA * pressure
    return jnp.abs(normal) + jnp.abs(scaled) * lax.rsqrt(jnp.maximum(scaled * density, 1e-30))


def face_flux(low, high, direction):
    rho_l, rho_r, p_l, p_r = low(0), high(0), low(4), high(4)
    u_l = [low(1 + j) for j in range(3)]
    u_r = [high(1 + j) for j in range(3)]
    n_l, n_r = u_l[direction], u_r[direction]
    speed = jnp.maximum(wave_speed(n_l, p_l, rho_l), wave_speed(n_r, p_r, rho_r))
    a_l, a_r = 0.5 * (n_l + speed), 0.5 * (n_r - speed)
    m_l, m_r = rho_l * a_l, rho_r * a_r
    flux = [m_l + m_r]
    for j in range(3):
        f = m_l * u_l[j] + m_r * u_r[j]
        if j == direction:
            f = f + 0.5 * (p_l + p_r)
        flux.append(f)
    k_l = u_l[0] * u_l[0] + u_l[1] * u_l[1] + u_l[2] * u_l[2]
    k_r = u_r[0] * u_r[0] + u_r[1] * u_r[1] + u_r[2] * u_r[2]
    flux.append(
        p_l * (2.5 * a_l + 0.5 * n_l) + p_r * (2.5 * a_r + 0.5 * n_r) + 0.5 * (m_l * k_l + m_r * k_r)
    )
    for j in range(5, NV):
        flux.append(m_l * low(j) + m_r * high(j))
    return flux


def primitives(c):
    inverse = 1.0 / c[0]
    u = [c[j] * inverse for j in (1, 2, 3)]
    kinetic = 0.5 * (c[1] * u[0] + c[2] * u[1] + c[3] * u[2])
    return [c[0]] + u + [0.4 * (c[4] - kinetic)] + [c[j] * inverse for j in range(5, NV)]


def lane():
    return lax.broadcasted_iota(jnp.int32, (8, 128), 1)


def fill_weights(weights):
    a = lax.broadcasted_iota(jnp.int32, (128, 128), 0)
    b = lax.broadcasted_iota(jnp.int32, (128, 128), 1)
    ga, gb, za, zb = a // NZ, b // NZ, a % NZ, b % NZ
    for slot in range(4):
        if slot == 3:
            offset = jnp.where(ga == gb, (za - zb + 3 + NZ) % NZ, NZ)
        else:
            offset = jnp.where(za == zb, 4 * (slot - 1) + ga - gb + 3, NZ)
        for side, coefficients in enumerate((LOW, HIGH)):
            w = jnp.zeros((128, 128), jnp.float32)
            for m, c in enumerate(coefficients):
                if c:
                    w = jnp.where(offset == m, c, w)
            w = w.astype(jnp.bfloat16)
            weights[slot, 0:128, 128 * side : 128 * side + 128] = w
            weights[slot, 128:256, 128 * side : 128 * side + 128] = w


def split_tile(q, qb, t):
    x = q[:, t, 3:19, :].reshape(NV * 16, 128) * (1.0 / 60.0)
    top = x.astype(jnp.bfloat16)
    qb[t, :, 0:128] = top
    qb[t, :, 128:256] = (x - top.astype(jnp.float32)).astype(jnp.bfloat16)


def dot(a, b):
    return jnp.dot(a, b, preferred_element_type=jnp.float32)


def store_primitives(q, t, row, c):
    for v, value in enumerate(primitives(c)):
        q[v, t, row : row + 8, :] = value


def inner_terms(q, qb, fs, fx, s, weights, rate):
    pre, act, heat = rate
    for t in (1, 2):
        split_tile(q, qb, t)
        fs[t - 1] = dot(qb[t], weights[3])
    first = lane() % NZ == NZ - 1

    def half(h, _):
        for kt in range(2):
            rows = slice(8 * kt, 8 * kt + 8)
            cells = slice(8 * kt + 3, 8 * kt + 11)
            stencil = [
                [q[v, h + 1, 8 * kt + m : 8 * kt + m + 8, :] for m in range(6)] for v in range(NV)
            ]
            pairs = [stencil_pair(x) for x in stencil]
            for v, f in enumerate(face_flux(lambda v: pairs[v][0], lambda v: pairs[v][1], 0)):
                fx[v, h, rows, :] = f
        for kt in range(2):
            rows = slice(8 * kt, 8 * kt + 8)
            cells = slice(8 * kt + 3, 8 * kt + 11)
            rho, pressure = q[0, h + 1, cells, :], q[4, h + 1, cells, :]
            ratio = rho / pressure
            rates = [
                pre[r] * rho * q[5 + r, h + 1, cells, :] * jnp.exp(-act[r] * ratio) for r in range(NR)
            ]
            release = heat[0] * rates[0]
            for r in range(1, NR):
                release = release + heat[r] * rates[r]
            source = [None] * 4 + [release, -rates[0]]
            source += [rates[r - 1] - rates[r] for r in range(1, NR)] + [rates[NR - 1]]
            flux = face_flux(
                lambda v: fs[h, 16 * v + 8 * kt : 16 * v + 8 * kt + 8, 0:128],
                lambda v: fs[h, 16 * v + 8 * kt : 16 * v + 8 * kt + 8, 128:256],
                2,
            )
            for v, f in enumerate(flux):
                above = jnp.where(first, pltpu.roll(f, NZ - 1, 1), pltpu.roll(f, 127, 1))
                x = (f - above) + (fx[v, h, rows, :] - fx[v, h, 8 * kt + 1 : 8 * kt + 9, :])
                if source[v] is not None:
                    x = x + source[v]
                s[v, h, rows, :] = x
        return 0

    lax.fori_loop(0, 2, half, 0)


def row_terms(q, qb, fs, fy, weights):
    split_tile(q, qb, 0)
    split_tile(q, qb, 3)
    for j in range(3):
        x = dot(qb[j], weights[0]) + dot(qb[j + 1], weights[1])
        if j < 2:
            x = x + dot(qb[j + 2], weights[2])
        fs[j] = x

    def tile(j, _):
        for kt in range(2):
            flux = face_flux(
                lambda v: fs[j, 16 * v + 8 * kt : 16 * v + 8 * kt + 8, 0:128],
                lambda v: fs[j, 16 * v + 8 * kt : 16 * v + 8 * kt + 8, 128:256],
                1,
            )
            for v, f in enumerate(flux):
                fy[v, j, 8 * kt : 8 * kt + 8, :] = f
        return 0

    lax.fori_loop(0, 3, tile, 0)


def rate_of(s, fy, v, h, kt):
    rows = slice(8 * kt, 8 * kt + 8)
    f = fy[v, h, rows, :]
    last = lane() >= 96
    above = jnp.where(last, pltpu.roll(fy[v, h + 1, rows, :], 96, 1), pltpu.roll(f, 96, 1))
    return s[v, h, rows, :] + (f - above)


def mirrored(x, sign):
    group = lane() // NZ
    return sign * jnp.where(group % 2 == 0, pltpu.roll(x, 32, 1), pltpu.roll(x, 96, 1))


def kernel(n_gx, n_gy, u, fresh_in, slide, cuts_in, pre_in, act_in, heat_in, out, us, fresh, cuts, pre, act, heat, xw, yl, yh, fb, yf, vw, xs, xl, xg, yl2, yh2,
           q, qb, fs, fx, fy, s, weights, send_sem, recv_sem, load_sem):
    gx, gy = lax.axis_index("gx"), lax.axis_index("gy")
    has_prev, has_next = gx > 0, gx < n_gx - 1
    has_below, has_above = gy > 0, gy < n_gy - 1
    inside = {-1: has_prev, 1: has_next}
    beside = {-1: has_below, 1: has_above}
    pairs = ((u, us), (fresh_in, fresh), (cuts_in, cuts), (pre_in, pre), (act_in, act), (heat_in, heat))
    loads = [pltpu.make_async_copy(a, b, load_sem.at[k]) for k, (a, b) in enumerate(pairs)]

    def both(a, b):
        return jnp.logical_and(a, b)

    def reach(dx, dy):
        if dx and dy:
            return both(inside[dx], beside[dy])
        return inside[dx] if dx else beside[dy]

    neighbours = [(a, b) for a in (-1, 0, 1) for b in (-1, 0, 1) if a or b]
    barrier = pltpu.get_barrier_semaphore()
    for dx, dy in neighbours:

        @pl.when(reach(dx, dy))
        def _(dx=dx, dy=dy):
            pl.semaphore_signal(barrier, inc=1, device_id=(gx + dx, gy + dy), device_id_type=MESH)

    for load in loads:
        load.start()
    for load in loads:
        load.wait()
    base = jnp.clip(cuts[gx] - gx * PX + slide[0], -2, 9)
    count = jnp.clip(cuts[gx + 1] - cuts[gx], 9, CAP)
    for p in range(PX):
        for h in range(2):
            xw[h, OWN + NV * p : OWN + NV * (p + 1), :] = us[p, :, 128 * h : 128 * h + 128]
    for h in range(2):
        fb[h, 0:NV, :] = fresh[:, 128 * h : 128 * h + 128]
        fb[h, NV:16, :] = jnp.zeros((2, 128), jnp.float32)
    along = 1 + jnp.where(has_prev, 1, 0) + jnp.where(has_next, 1, 0)
    across = 1 + jnp.where(has_below, 1, 0) + jnp.where(has_above, 1, 0)
    pl.semaphore_wait(barrier, along * across - 1)

    def remote(k, src, dst, dx, dy):
        return pltpu.make_async_remote_copy(
            src_ref=src, dst_ref=dst, send_sem=send_sem.at[k], recv_sem=recv_sem.at[k],
            device_id=(gx + dx, gy + dy), device_id_type=MESH,
        )

    x_first = [
        (has_prev, remote(0, xw.at[:, OWN:NEXT], xw.at[:, NEXT : NEXT + PX * NV], -1, 0), has_next),
        (has_next, remote(1, xw.at[:, OWN + 96 : NEXT], xw.at[:, 40:OWN], 1, 0), has_prev),
    ]
    y_first = []
    for k, (dy, h, ghost) in enumerate(((1, 1, yl), (-1, 0, yh))):
        to, of = beside[dy], beside[-dy]
        y_first.append((to, remote(2 + 4 * k, xw.at[h, OWN:NEXT], ghost.at[Y_OWN:Y_NEXT], 0, dy), of))
        y_first.append((
            both(to, has_prev),
            remote(3 + 4 * k, xw.at[h, OWN : OWN + 128], ghost.at[Y_NEXT : Y_NEXT + 128], -1, dy),
            both(of, has_next),
        ))
        y_first.append((
            both(to, has_next),
            remote(4 + 4 * k, xw.at[h, OWN + 136 : NEXT], ghost.at[Y_OWN - 32 : Y_OWN], 1, dy),
            both(of, has_prev),
        ))
        y_first.append((
            both(to, jnp.logical_not(has_next)),
            remote(5 + 4 * k, fb.at[h], yf.at[k], 0, dy),
            both(of, jnp.logical_not(has_next)),
        ))

    def start(copies):
        for to, copy, _ in copies:

            @pl.when(to)
            def _(copy=copy):
                copy.start()

    def arrive(copies):
        for _, copy, of in copies:

            @pl.when(of)
            def _(copy=copy):
                copy.wait_recv()

    def leave(copies):
        for to, copy, _ in copies:

            @pl.when(to)
            def _(copy=copy):
                copy.wait_send()

    start(x_first)
    start(y_first)
    fill_weights(weights)
    row_id = lax.broadcasted_iota(jnp.int32, (8, 128), 0)

    arrive(x_first)

    @pl.when(jnp.logical_not(has_next))
    def _():
        for p in range(12, 27):
            for h in range(2):
                xw[h, OWN + NV * p : OWN + NV * (p + 1), :] = fb[h, 0:NV, :]

    def window(h, k, v):
        return xw[h, pl.ds((base + 8 + k) * NV + v, 8, stride=NV), :]

    low_edge = both(jnp.logical_not(has_prev), row_id < 3)

    def window_tile(h, _):
        for j in range(3):
            c = [window(h, 8 * j - 3, v) for v in range(NV)]
            if j == 0:
                c = [jnp.where(low_edge, xw[h, pl.ds((base + 8) * NV + v, 1), :], c[v]) for v in range(NV)]
            store_primitives(q, h + 1, 8 * j, c)
        return 0

    lax.fori_loop(0, 2, window_tile, 0)
    inner_terms(q, qb, fs, fx, s, weights, (pre, act, heat))

    arrive(y_first)

    @pl.when(jnp.logical_not(has_next))
    def _():
        for p in range(12, 21):
            for ghost, k in ((yl, 0), (yh, 1)):
                ghost[Y_OWN + NV * p : Y_OWN + NV * (p + 1), :] = yf[k, 0:NV, :]

    for t, h, ghost, is_wall in ((0, 0, yl, jnp.logical_not(has_below)), (3, 1, yh, jnp.logical_not(has_above))):
        for kt in range(2):

            @pl.when(is_wall)
            def _(t=t, h=h, kt=kt):
                c = [mirrored(window(h, 8 * kt, v), -1.0 if v == 2 else 1.0) for v in range(NV)]
                store_primitives(q, t, 8 * kt + 3, c)

            @pl.when(jnp.logical_not(is_wall))
            def _(t=t, ghost=ghost, kt=kt):
                c = [ghost[pl.ds((base + 4 + 8 * kt) * NV + v, 8, stride=NV), :] for v in range(NV)]
                store_primitives(q, t, 8 * kt + 3, c)

    row_terms(q, qb, fs, fy, weights)

    def first_update(h, _):
        for kt in range(2):
            for v in range(NV):
                x = window(h, 8 * kt, v) + TIME_STEP * rate_of(s, fy, v, h, kt)
                vw[h, pl.ds(V_OWN + 8 * kt * NV + v, 8, stride=NV), :] = x
        return 0

    lax.fori_loop(0, 2, first_update, 0)

    for h in range(2):
        xs[h] = vw[h, pl.ds(V_OWN + (count - 3) * NV - 6, 48), :]
    second = [
        (has_prev, remote(10, vw.at[:, V_OWN : V_OWN + 48], xg.at[:, G_OWN : G_OWN + 48], -1, 0), has_next),
        (has_next, remote(11, xs, xl.at[:, 0:48], 1, 0), has_prev),
    ]
    y_second = [
        (has_above, remote(12, vw.at[1, V_OWN : V_OWN + 216], yl2.at[0:216], 0, 1), has_below),
        (has_below, remote(13, vw.at[0, V_OWN : V_OWN + 216], yh2.at[0:216], 0, -1), has_above),
    ]
    start(second)
    start(y_second)

    @pl.when(jnp.logical_not(has_next))
    def _():
        for p in range(3):
            for h in range(2):
                xg[h, G_OWN + NV * p : G_OWN + NV * (p + 1), :] = fb[h, 0:NV, :]

    arrive(second)

    def second_tile(h, _):
        for j in range(3):
            k = 8 * j - 3
            c = [vw[h, pl.ds(V_OWN + k * NV + v, 8, stride=NV), :] for v in range(NV)]
            if j == 0:
                ghosts = [xl[h, pl.ds(6 + v, 8, stride=NV), :] for v in range(NV)]
                c = [jnp.where(row_id < 3, ghosts[v], c[v]) for v in range(NV)]
                c = [jnp.where(low_edge, vw[h, V_OWN + v : V_OWN + v + 1, :], c[v]) for v in range(NV)]
            else:
                owned = row_id + k < count
                c = [
                    jnp.where(owned, c[v], xg[h, pl.ds(G_OWN + (k - count) * NV + v, 8, stride=NV), :])
                    for v in range(NV)
                ]
            store_primitives(q, h + 1, 8 * j, c)
        return 0

    lax.fori_loop(0, 2, second_tile, 0)
    inner_terms(q, qb, fs, fx, s, weights, (pre, act, heat))

    arrive(y_second)
    for t, h, ghost, is_wall in ((0, 0, yl2, jnp.logical_not(has_below)), (3, 1, yh2, jnp.logical_not(has_above))):
        for kt in range(2):

            @pl.when(is_wall)
            def _(t=t, h=h, kt=kt):
                c = [
                    mirrored(vw[h, pl.ds(V_OWN + 8 * kt * NV + v, 8, stride=NV), :], -1.0 if v == 2 else 1.0)
                    for v in range(NV)
                ]
                store_primitives(q, t, 8 * kt + 3, c)

            @pl.when(jnp.logical_not(is_wall))
            def _(t=t, ghost=ghost, kt=kt):
                c = [ghost[pl.ds(8 * kt * NV + v, 8, stride=NV), :] for v in range(NV)]
                store_primitives(q, t, 8 * kt + 3, c)

    row_terms(q, qb, fs, fy, weights)
    for h in range(2):
        for kt in range(2):
            owned = row_id + 8 * kt < count
            for v in range(NV):
                w = window(h, 8 * kt, v)
                x = vw[h, pl.ds(V_OWN + 8 * kt * NV + v, 8, stride=NV), :] + TIME_STEP * rate_of(s, fy, v, h, kt)
                x = jnp.where(owned, 0.75 * w + 0.25 * x, 0.0)
                if kt == 0:
                    out[v, 0:8, 128 * h : 128 * h + 128] = x
                else:
                    out[v, 8:CAP, 128 * h : 128 * h + 128] = x[0 : CAP - 8]

    leave(x_first)
    leave(y_first)
    leave(second)
    leave(y_second)


def body(n_gx, n_gy, gas_state, inflow, slide_count, cut_list, prefactor, activation, heat_release):
    def f32(*shape):
        return pltpu.VMEM(shape, jnp.float32)

    return pl.pallas_call(
        functools.partial(kernel, n_gx, n_gy),
        out_shape=pltpu.VMEM((NV, CAP, 256), jnp.float32),
        in_specs=[pl.BlockSpec(memory_space=m) for m in [pltpu.HBM] * 2 + [pltpu.SMEM] + [pltpu.HBM] * 4],
        out_specs=pl.BlockSpec(memory_space=pltpu.VMEM),
        scratch_shapes=[
            f32(PX, NV, 256),
            f32(NV, 256),
            pltpu.SMEM((n_gx + 1,), jnp.int32),
            pltpu.SMEM((NR,), jnp.float32),
            pltpu.SMEM((NR,), jnp.float32),
            pltpu.SMEM((NR,), jnp.float32),
            f32(2, W_ROWS, 128),
            f32(Y_ROWS, 128),
            f32(Y_ROWS, 128),
            f32(2, 16, 128),
            f32(2, 16, 128),
            f32(2, V_ROWS, 128),
            f32(2, 48, 128),
            f32(2, 136, 128),
            f32(2, G_ROWS, 128),
            f32(240, 128),
            f32(240, 128),
            f32(NV, 4, 24, 128),
            pltpu.VMEM((4, NV * 16, 256), jnp.bfloat16),
            f32(3, NV * 16, 256),
            f32(NV, 2, 24, 128),
            f32(NV, 3, 16, 128),
            f32(NV, 2, 16, 128),
            pltpu.VMEM((4, 256, 256), jnp.bfloat16),
            pltpu.SemaphoreType.DMA((14,)),
            pltpu.SemaphoreType.DMA((14,)),
            pltpu.SemaphoreType.DMA((6,)),
        ],
        compiler_params=pltpu.CompilerParams(
            collective_id=0, has_side_effects=True, vmem_limit_bytes=32 * 1024 * 1024
        ),
        name="two_stages",
    )(*[
        x if x is slide_count else pltpu.with_memory_space_constraint(x, pltpu.HBM)
        for x in (
            jnp.transpose(gas_state, (1, 0, 2)), inflow, slide_count, cut_list, prefactor, activation, heat_release
        )
    ])


def solution(mesh):
    in_specs = (P(None, "gx", "gy"), P(None, "gy"), P(), P(), P(), P(), P())
    return jax.shard_map(
        functools.partial(body, mesh.shape["gx"], mesh.shape["gy"]),
        mesh=mesh,
        in_specs=in_specs,
        out_specs=P(None, "gx", "gy"),
        check_vma=False,
    )
```

```python
import functools

import jax
import jax.numpy as jnp
from jax import lax
from jax.experimental import pallas as pl
from jax.experimental.pallas import tpu as pltpu
from jax.sharding import PartitionSpec as P

MESH = pl.DeviceIdType.MESH
NV = 14
NR = 8
PX = 12
CAP = 15
NZ = 32
GAS_GAMMA = 1.4
TIME_STEP = 0.025

OWN = 8 * NV
NEXT = OWN + PX * NV
Y_OWN = 4 * NV
Y_NEXT = Y_OWN + PX * NV
V_OWN = 4 * NV
G_OWN = 12 * NV

PARTS = ((0, 42, 0), (0, 32, 128), (136, 8, 224))

W_ROWS = 560
Y_ROWS = 424
V_ROWS = 56 + 24 * NV
G_ROWS = 352

LOW = (2.0, -13.0, 47.0, 27.0, -3.0, 0.0)
HIGH = (0.0, -3.0, 27.0, 47.0, -13.0, 2.0)


def stencil_pair(q):
    d = [c / 60.0 for c in (2.0, 13.0, 47.0, 27.0, 3.0)]
    low = (d[0] * q[0] - d[1] * q[1]) + (d[2] * q[2] + d[3] * q[3]) - d[4] * q[4]
    high = (d[3] * q[2] - d[4] * q[1]) + (d[2] * q[3] - d[1] * q[4]) + d[0] * q[5]
    return low, high


def wave_speed(normal, pressure, density):
    scaled = GAS_GAMMA * pressure
    return jnp.abs(normal) + jnp.abs(scaled) * lax.rsqrt(jnp.maximum(scaled * density, 1e-30))


def face_flux(low, high, direction):
    rho_l, rho_r, p_l, p_r = low(0), high(0), low(4), high(4)
    u_l = [low(1 + j) for j in range(3)]
    u_r = [high(1 + j) for j in range(3)]
    n_l, n_r = u_l[direction], u_r[direction]
    speed = jnp.maximum(wave_speed(n_l, p_l, rho_l), wave_speed(n_r, p_r, rho_r))
    a_l, a_r = 0.5 * (n_l + speed), 0.5 * (n_r - speed)
    m_l, m_r = rho_l * a_l, rho_r * a_r
    flux = [m_l + m_r]
    for j in range(3):
        f = m_l * u_l[j] + m_r * u_r[j]
        if j == direction:
            f = f + 0.5 * (p_l + p_r)
        flux.append(f)
    k_l = u_l[0] * u_l[0] + u_l[1] * u_l[1] + u_l[2] * u_l[2]
    k_r = u_r[0] * u_r[0] + u_r[1] * u_r[1] + u_r[2] * u_r[2]
    flux.append(
        p_l * (2.5 * a_l + 0.5 * n_l) + p_r * (2.5 * a_r + 0.5 * n_r) + 0.5 * (m_l * k_l + m_r * k_r)
    )
    for j in range(5, NV):
        flux.append(m_l * low(j) + m_r * high(j))
    return flux


def primitives(c):
    inverse = 1.0 / c[0]
    u = [c[j] * inverse for j in (1, 2, 3)]
    kinetic = 0.5 * (c[1] * u[0] + c[2] * u[1] + c[3] * u[2])
    return [c[0]] + u + [0.4 * (c[4] - kinetic)] + [c[j] * inverse for j in range(5, NV)]


def lane():
    return lax.broadcasted_iota(jnp.int32, (8, 128), 1)


def fill_weights(weights):
    a = lax.broadcasted_iota(jnp.int32, (128, 128), 0)
    b = lax.broadcasted_iota(jnp.int32, (128, 128), 1)
    ga, gb, za, zb = a // NZ, b // NZ, a % NZ, b % NZ
    for slot in range(4):
        if slot == 3:
            offset = jnp.where(ga == gb, (za - zb + 3 + NZ) % NZ, NZ)
        else:
            offset = jnp.where(za == zb, 4 * (slot - 1) + ga - gb + 3, NZ)
        for side, coefficients in enumerate((LOW, HIGH)):
            w = jnp.zeros((128, 128), jnp.float32)
            for m, c in enumerate(coefficients):
                if c:
                    w = jnp.where(offset == m, c, w)
            w = w.astype(jnp.bfloat16)
            weights[slot, 0:128, 128 * side : 128 * side + 128] = w
            weights[slot, 128:256, 128 * side : 128 * side + 128] = w


def split_tile(q, qb, t):
    x = q[:, t, 3:19, :].reshape(NV * 16, 128) * (1.0 / 60.0)
    top = x.astype(jnp.bfloat16)
    qb[t, :, 0:128] = top
    qb[t, :, 128:256] = (x - top.astype(jnp.float32)).astype(jnp.bfloat16)


def dot(a, b):
    return jnp.dot(a, b, preferred_element_type=jnp.float32)


def store_primitives(q, t, row, c):
    for v, value in enumerate(primitives(c)):
        q[v, t, row : row + 8, :] = value


def inner_terms(q, qb, fs, fx, s, weights, rate):
    pre, act, heat = rate
    for t in (1, 2):
        split_tile(q, qb, t)
        fs[t - 1] = dot(qb[t], weights[3])
    first = lane() % NZ == NZ - 1

    def half(h, _):
        for kt in range(2):
            rows = slice(8 * kt, 8 * kt + 8)
            cells = slice(8 * kt + 3, 8 * kt + 11)
            stencil = [
                [q[v, h + 1, 8 * kt + m : 8 * kt + m + 8, :] for m in range(6)] for v in range(NV)
            ]
            pairs = [stencil_pair(x) for x in stencil]
            for v, f in enumerate(face_flux(lambda v: pairs[v][0], lambda v: pairs[v][1], 0)):
                fx[v, h, rows, :] = f
        for kt in range(2):
            rows = slice(8 * kt, 8 * kt + 8)
            cells = slice(8 * kt + 3, 8 * kt + 11)
            rho, pressure = q[0, h + 1, cells, :], q[4, h + 1, cells, :]
            ratio = rho / pressure
            rates = [
                pre[r] * rho * q[5 + r, h + 1, cells, :] * jnp.exp(-act[r] * ratio) for r in range(NR)
            ]
            release = heat[0] * rates[0]
            for r in range(1, NR):
                release = release + heat[r] * rates[r]
            source = [None] * 4 + [release, -rates[0]]
            source += [rates[r - 1] - rates[r] for r in range(1, NR)] + [rates[NR - 1]]
            flux = face_flux(
                lambda v: fs[h, 16 * v + 8 * kt : 16 * v + 8 * kt + 8, 0:128],
                lambda v: fs[h, 16 * v + 8 * kt : 16 * v + 8 * kt + 8, 128:256],
                2,
            )
            for v, f in enumerate(flux):
                above = jnp.where(first, pltpu.roll(f, NZ - 1, 1), pltpu.roll(f, 127, 1))
                x = (f - above) + (fx[v, h, rows, :] - fx[v, h, 8 * kt + 1 : 8 * kt + 9, :])
                if source[v] is not None:
                    x = x + source[v]
                s[v, h, rows, :] = x
        return 0

    lax.fori_loop(0, 2, half, 0)


def row_terms(q, qb, fs, fy, weights):
    split_tile(q, qb, 0)
    split_tile(q, qb, 3)
    for j in range(3):
        x = dot(qb[j], weights[0]) + dot(qb[j + 1], weights[1])
        if j < 2:
            x = x + dot(qb[j + 2], weights[2])
        fs[j] = x

    def tile(j, _):
        for kt in range(2):
            flux = face_flux(
                lambda v: fs[j, 16 * v + 8 * kt : 16 * v + 8 * kt + 8, 0:128],
                lambda v: fs[j, 16 * v + 8 * kt : 16 * v + 8 * kt + 8, 128:256],
                1,
            )
            for v, f in enumerate(flux):
                fy[v, j, 8 * kt : 8 * kt + 8, :] = f
        return 0

    lax.fori_loop(0, 3, tile, 0)


def rate_of(s, fy, v, h, kt):
    rows = slice(8 * kt, 8 * kt + 8)
    f = fy[v, h, rows, :]
    last = lane() >= 96
    above = jnp.where(last, pltpu.roll(fy[v, h + 1, rows, :], 96, 1), pltpu.roll(f, 96, 1))
    return s[v, h, rows, :] + (f - above)


def mirrored(x, sign):
    group = lane() // NZ
    return sign * jnp.where(group % 2 == 0, pltpu.roll(x, 32, 1), pltpu.roll(x, 96, 1))


def pack(src, start, quarter, dst, to, free):
    group = lax.broadcasted_iota(jnp.int32, (quarter, 128), 1) // NZ
    last = src(start + 3 * quarter, quarter)
    for j in range(3):
        moved = pltpu.roll(last, (32 * (3 - j) if free == 3 else 128 - 32 * (j + 1)), 1)
        dst[to + j * quarter : to + (j + 1) * quarter, :] = jnp.where(
            group == free, moved, src(start + j * quarter, quarter)
        )


def unpack(src, start, quarter, dst, to, free):
    group = lax.broadcasted_iota(jnp.int32, (quarter, 128), 1) // NZ
    last = jnp.ones((quarter, 128), jnp.float32)
    for j in range(3):
        x = src[start + j * quarter : start + (j + 1) * quarter, :]
        dst[to + j * quarter : to + (j + 1) * quarter, :] = jnp.where(group == free, 1.0, x)
        last = jnp.where(group == (j if free == 3 else j + 1), pltpu.roll(x, 32 * (j + 1), 1), last)
    dst[to + 3 * quarter : to + 4 * quarter, :] = last


def kernel(n_gx, n_gy, u, fresh_in, slide, cuts_in, pre_in, act_in, heat_in, out, us, fresh, cuts, pre, act, heat, xw, yl, yh, fb, yf, vw, xs, xl, xg, yl2, yh2, ps, yp, ps2, yp2,
           q, qb, fs, fx, fy, s, weights, send_sem, recv_sem, load_sem):
    gx, gy = lax.axis_index("gx"), lax.axis_index("gy")
    has_prev, has_next = gx > 0, gx < n_gx - 1
    has_below, has_above = gy > 0, gy < n_gy - 1
    inside = {-1: has_prev, 1: has_next}
    beside = {-1: has_below, 1: has_above}
    pairs = ((u, us), (fresh_in, fresh), (cuts_in, cuts), (pre_in, pre), (act_in, act), (heat_in, heat))
    loads = [pltpu.make_async_copy(a, b, load_sem.at[k]) for k, (a, b) in enumerate(pairs)]

    def both(a, b):
        return jnp.logical_and(a, b)

    def reach(dx, dy):
        if dx and dy:
            return both(inside[dx], beside[dy])
        return inside[dx] if dx else beside[dy]

    neighbours = [(a, b) for a in (-1, 0, 1) for b in (-1, 0, 1) if a or b]
    barrier = pltpu.get_barrier_semaphore()
    for dx, dy in neighbours:

        @pl.when(reach(dx, dy))
        def _(dx=dx, dy=dy):
            pl.semaphore_signal(barrier, inc=1, device_id=(gx + dx, gy + dy), device_id_type=MESH)

    for load in loads:
        load.start()
    for load in loads:
        load.wait()
    base = jnp.clip(cuts[gx] - gx * PX + slide[0], -2, 9)
    count = jnp.clip(cuts[gx + 1] - cuts[gx], 9, CAP)
    for p in range(PX):
        for h in range(2):
            xw[h, OWN + NV * p : OWN + NV * (p + 1), :] = us[p, :, 128 * h : 128 * h + 128]
    for h in range(2):
        fb[h, 0:NV, :] = fresh[:, 128 * h : 128 * h + 128]
        fb[h, NV:16, :] = jnp.zeros((2, 128), jnp.float32)
    for k, h in ((0, 1), (1, 0)):
        for row, quarter, to in PARTS:
            pack(lambda a, n, h=h: xw[h, a : a + n, :], OWN + row, quarter, ps.at[k], to, 3 * k)
    along = 1 + jnp.where(has_prev, 1, 0) + jnp.where(has_next, 1, 0)
    across = 1 + jnp.where(has_below, 1, 0) + jnp.where(has_above, 1, 0)
    pl.semaphore_wait(barrier, along * across - 1)

    def remote(k, src, dst, dx, dy):
        return pltpu.make_async_remote_copy(
            src_ref=src, dst_ref=dst, send_sem=send_sem.at[k], recv_sem=recv_sem.at[k],
            device_id=(gx + dx, gy + dy), device_id_type=MESH,
        )

    x_first = [
        (has_prev, remote(0, xw.at[:, OWN:NEXT], xw.at[:, NEXT : NEXT + PX * NV], -1, 0), has_next),
        (has_next, remote(1, xw.at[:, OWN + 96 : NEXT], xw.at[:, 40:OWN], 1, 0), has_prev),
    ]
    y_first = []
    for k, dy in enumerate((1, -1)):
        to, of = beside[dy], beside[-dy]
        y_first.append((to, remote(2 + 4 * k, ps.at[k, 0:128], yp.at[k, 0:128], 0, dy), of))
        y_first.append((
            both(to, has_prev),
            remote(3 + 4 * k, ps.at[k, 128:224], yp.at[k, 128:224], -1, dy),
            both(of, has_next),
        ))
        y_first.append((
            both(to, has_next),
            remote(4 + 4 * k, ps.at[k, 224:248], yp.at[k, 224:248], 1, dy),
            both(of, has_prev),
        ))
        y_first.append((
            both(to, jnp.logical_not(has_next)),
            remote(5 + 4 * k, fb.at[1 - k], yf.at[k], 0, dy),
            both(of, jnp.logical_not(has_next)),
        ))

    def start(copies):
        for to, copy, _ in copies:

            @pl.when(to)
            def _(copy=copy):
                copy.start()

    def arrive(copies):
        for _, copy, of in copies:

            @pl.when(of)
            def _(copy=copy):
                copy.wait_recv()

    def leave(copies):
        for to, copy, _ in copies:

            @pl.when(to)
            def _(copy=copy):
                copy.wait_send()

    start(x_first)
    start(y_first)
    fill_weights(weights)
    row_id = lax.broadcasted_iota(jnp.int32, (8, 128), 0)

    arrive(x_first)

    @pl.when(jnp.logical_not(has_next))
    def _():
        for p in range(12, 27):
            for h in range(2):
                xw[h, OWN + NV * p : OWN + NV * (p + 1), :] = fb[h, 0:NV, :]

    def window(h, k, v):
        return xw[h, pl.ds((base + 8 + k) * NV + v, 8, stride=NV), :]

    low_edge = both(jnp.logical_not(has_prev), row_id < 3)

    def window_tile(h, _):
        for j in range(3):
            c = [window(h, 8 * j - 3, v) for v in range(NV)]
            if j == 0:
                c = [jnp.where(low_edge, xw[h, pl.ds((base + 8) * NV + v, 1), :], c[v]) for v in range(NV)]
            store_primitives(q, h + 1, 8 * j, c)
        return 0

    lax.fori_loop(0, 2, window_tile, 0)
    inner_terms(q, qb, fs, fx, s, weights, (pre, act, heat))

    arrive(y_first)
    for k, ghost in ((0, yl), (1, yh)):
        for (_, quarter, row), to in zip(PARTS, (Y_OWN, Y_NEXT, Y_OWN - 32)):
            unpack(yp.at[k], row, quarter, ghost, to, 3 * k)

    @pl.when(jnp.logical_not(has_next))
    def _():
        for p in range(12, 21):
            for ghost, k in ((yl, 0), (yh, 1)):
                ghost[Y_OWN + NV * p : Y_OWN + NV * (p + 1), :] = yf[k, 0:NV, :]

    for t, h, ghost, is_wall in ((0, 0, yl, jnp.logical_not(has_below)), (3, 1, yh, jnp.logical_not(has_above))):
        for kt in range(2):

            @pl.when(is_wall)
            def _(t=t, h=h, kt=kt):
                c = [mirrored(window(h, 8 * kt, v), -1.0 if v == 2 else 1.0) for v in range(NV)]
                store_primitives(q, t, 8 * kt + 3, c)

            @pl.when(jnp.logical_not(is_wall))
            def _(t=t, ghost=ghost, kt=kt):
                c = [ghost[pl.ds((base + 4 + 8 * kt) * NV + v, 8, stride=NV), :] for v in range(NV)]
                store_primitives(q, t, 8 * kt + 3, c)

    row_terms(q, qb, fs, fy, weights)

    def first_update(h, _):
        for kt in range(2):
            for v in range(NV):
                x = window(h, 8 * kt, v) + TIME_STEP * rate_of(s, fy, v, h, kt)
                vw[h, pl.ds(V_OWN + 8 * kt * NV + v, 8, stride=NV), :] = x
        return 0

    lax.fori_loop(0, 2, first_update, 0)

    for h in range(2):
        xs[h] = vw[h, pl.ds(V_OWN + (count - 3) * NV - 6, 48), :]
    second = [
        (has_prev, remote(10, vw.at[:, V_OWN : V_OWN + 48], xg.at[:, G_OWN : G_OWN + 48], -1, 0), has_next),
        (has_next, remote(11, xs, xl.at[:, 0:48], 1, 0), has_prev),
    ]
    y_second = [
        (has_above, remote(12, ps2.at[0], yp2.at[0], 0, 1), has_below),
        (has_below, remote(13, ps2.at[1], yp2.at[1], 0, -1), has_above),
    ]
    start(second)
    for k, h in ((0, 1), (1, 0)):
        pack(lambda a, n, h=h: vw[h, a : a + n, :], V_OWN, 56, ps2.at[k], 0, 3 * k)
    start(y_second)

    @pl.when(jnp.logical_not(has_next))
    def _():
        for p in range(3):
            for h in range(2):
                xg[h, G_OWN + NV * p : G_OWN + NV * (p + 1), :] = fb[h, 0:NV, :]

    arrive(second)

    def second_tile(h, _):
        for j in range(3):
            k = 8 * j - 3
            c = [vw[h, pl.ds(V_OWN + k * NV + v, 8, stride=NV), :] for v in range(NV)]
            if j == 0:
                ghosts = [xl[h, pl.ds(6 + v, 8, stride=NV), :] for v in range(NV)]
                c = [jnp.where(row_id < 3, ghosts[v], c[v]) for v in range(NV)]
                c = [jnp.where(low_edge, vw[h, V_OWN + v : V_OWN + v + 1, :], c[v]) for v in range(NV)]
            else:
                owned = row_id + k < count
                c = [
                    jnp.where(owned, c[v], xg[h, pl.ds(G_OWN + (k - count) * NV + v, 8, stride=NV), :])
                    for v in range(NV)
                ]
            store_primitives(q, h + 1, 8 * j, c)
        return 0

    lax.fori_loop(0, 2, second_tile, 0)
    inner_terms(q, qb, fs, fx, s, weights, (pre, act, heat))

    arrive(y_second)
    for k, ghost in ((0, yl2), (1, yh2)):
        unpack(yp2.at[k], 0, 56, ghost, 0, 3 * k)
    for t, h, ghost, is_wall in ((0, 0, yl2, jnp.logical_not(has_below)), (3, 1, yh2, jnp.logical_not(has_above))):
        for kt in range(2):

            @pl.when(is_wall)
            def _(t=t, h=h, kt=kt):
                c = [
                    mirrored(vw[h, pl.ds(V_OWN + 8 * kt * NV + v, 8, stride=NV), :], -1.0 if v == 2 else 1.0)
                    for v in range(NV)
                ]
                store_primitives(q, t, 8 * kt + 3, c)

            @pl.when(jnp.logical_not(is_wall))
            def _(t=t, ghost=ghost, kt=kt):
                c = [ghost[pl.ds(8 * kt * NV + v, 8, stride=NV), :] for v in range(NV)]
                store_primitives(q, t, 8 * kt + 3, c)

    row_terms(q, qb, fs, fy, weights)
    for h in range(2):
        for kt in range(2):
            owned = row_id + 8 * kt < count
            for v in range(NV):
                w = window(h, 8 * kt, v)
                x = vw[h, pl.ds(V_OWN + 8 * kt * NV + v, 8, stride=NV), :] + TIME_STEP * rate_of(s, fy, v, h, kt)
                x = jnp.where(owned, 0.75 * w + 0.25 * x, 0.0)
                if kt == 0:
                    out[v, 0:8, 128 * h : 128 * h + 128] = x
                else:
                    out[v, 8:CAP, 128 * h : 128 * h + 128] = x[0 : CAP - 8]

    leave(x_first)
    leave(y_first)
    leave(second)
    leave(y_second)


def body(n_gx, n_gy, gas_state, inflow, slide_count, cut_list, prefactor, activation, heat_release):
    def f32(*shape):
        return pltpu.VMEM(shape, jnp.float32)

    return pl.pallas_call(
        functools.partial(kernel, n_gx, n_gy),
        out_shape=pltpu.VMEM((NV, CAP, 256), jnp.float32),
        in_specs=[pl.BlockSpec(memory_space=m) for m in [pltpu.HBM] * 2 + [pltpu.SMEM] + [pltpu.HBM] * 4],
        out_specs=pl.BlockSpec(memory_space=pltpu.VMEM),
        scratch_shapes=[
            f32(PX, NV, 256),
            f32(NV, 256),
            pltpu.SMEM((n_gx + 1,), jnp.int32),
            pltpu.SMEM((NR,), jnp.float32),
            pltpu.SMEM((NR,), jnp.float32),
            pltpu.SMEM((NR,), jnp.float32),
            f32(2, W_ROWS, 128),
            f32(Y_ROWS, 128),
            f32(Y_ROWS, 128),
            f32(2, 16, 128),
            f32(2, 16, 128),
            f32(2, V_ROWS, 128),
            f32(2, 48, 128),
            f32(2, 136, 128),
            f32(2, G_ROWS, 128),
            f32(240, 128),
            f32(240, 128),
            f32(2, 248, 128),
            f32(2, 248, 128),
            f32(2, 168, 128),
            f32(2, 168, 128),
            f32(NV, 4, 24, 128),
            pltpu.VMEM((4, NV * 16, 256), jnp.bfloat16),
            f32(3, NV * 16, 256),
            f32(NV, 2, 24, 128),
            f32(NV, 3, 16, 128),
            f32(NV, 2, 16, 128),
            pltpu.VMEM((4, 256, 256), jnp.bfloat16),
            pltpu.SemaphoreType.DMA((14,)),
            pltpu.SemaphoreType.DMA((14,)),
            pltpu.SemaphoreType.DMA((6,)),
        ],
        compiler_params=pltpu.CompilerParams(
            collective_id=0, has_side_effects=True, vmem_limit_bytes=32 * 1024 * 1024
        ),
        name="two_stages",
    )(*[
        x if x is slide_count else pltpu.with_memory_space_constraint(x, pltpu.HBM)
        for x in (
            jnp.transpose(gas_state, (1, 0, 2)), inflow, slide_count, cut_list, prefactor, activation, heat_release
        )
    ])


def solution(mesh):
    in_specs = (P(None, "gx", "gy"), P(None, "gy"), P(), P(), P(), P(), P())
    return jax.shard_map(
        functools.partial(body, mesh.shape["gx"], mesh.shape["gy"]),
        mesh=mesh,
        in_specs=in_specs,
        out_specs=P(None, "gx", "gy"),
        check_vma=False,
    )
```

```python
import functools

import jax
import jax.numpy as jnp
from jax import lax
from jax.experimental import pallas as pl
from jax.experimental.pallas import tpu as pltpu
from jax.sharding import PartitionSpec as P

MESH = pl.DeviceIdType.MESH
NV = 14
NR = 8
PX = 12
CAP = 15
NZ = 32
GAS_GAMMA = 1.4
TIME_STEP = 0.025

ORIGIN = 16
OWN = ORIGIN * NV
NEXT = OWN + PX * NV
Y_ORIGIN = 12
Y_OWN = Y_ORIGIN * NV
Y_NEXT = Y_OWN + PX * NV
V_OWN = 4 * NV
G_OWN = 12 * NV

PARTS = ((0, 42, 0), (0, 32, 128), (136, 8, 224))
RUN_PART = (96, 18, 248)
RUN = 32
ROW0 = 11

W_ROWS = 672
Y_ROWS = 544
V_ROWS = 56 + 24 * NV
G_ROWS = 352

LOW = (2.0, -13.0, 47.0, 27.0, -3.0, 0.0)
HIGH = (0.0, -3.0, 27.0, 47.0, -13.0, 2.0)


def stencil_pair(q):
    d = [c / 60.0 for c in (2.0, 13.0, 47.0, 27.0, 3.0)]
    low = (d[0] * q[0] - d[1] * q[1]) + (d[2] * q[2] + d[3] * q[3]) - d[4] * q[4]
    high = (d[3] * q[2] - d[4] * q[1]) + (d[2] * q[3] - d[1] * q[4]) + d[0] * q[5]
    return low, high


def wave_speed(normal, pressure, density):
    scaled = GAS_GAMMA * pressure
    return jnp.abs(normal) + jnp.abs(scaled) * lax.rsqrt(jnp.maximum(scaled * density, 1e-30))


def face_flux(low, high, direction):
    rho_l, rho_r, p_l, p_r = low(0), high(0), low(4), high(4)
    u_l = [low(1 + j) for j in range(3)]
    u_r = [high(1 + j) for j in range(3)]
    n_l, n_r = u_l[direction], u_r[direction]
    speed = jnp.maximum(wave_speed(n_l, p_l, rho_l), wave_speed(n_r, p_r, rho_r))
    a_l, a_r = 0.5 * (n_l + speed), 0.5 * (n_r - speed)
    m_l, m_r = rho_l * a_l, rho_r * a_r
    flux = [m_l + m_r]
    for j in range(3):
        f = m_l * u_l[j] + m_r * u_r[j]
        if j == direction:
            f = f + 0.5 * (p_l + p_r)
        flux.append(f)
    k_l = u_l[0] * u_l[0] + u_l[1] * u_l[1] + u_l[2] * u_l[2]
    k_r = u_r[0] * u_r[0] + u_r[1] * u_r[1] + u_r[2] * u_r[2]
    flux.append(
        p_l * (2.5 * a_l + 0.5 * n_l) + p_r * (2.5 * a_r + 0.5 * n_r) + 0.5 * (m_l * k_l + m_r * k_r)
    )
    for j in range(5, NV):
        flux.append(m_l * low(j) + m_r * high(j))
    return flux


def primitives(c):
    inverse = 1.0 / c[0]
    u = [c[j] * inverse for j in (1, 2, 3)]
    kinetic = 0.5 * (c[1] * u[0] + c[2] * u[1] + c[3] * u[2])
    return [c[0]] + u + [0.4 * (c[4] - kinetic)] + [c[j] * inverse for j in range(5, NV)]


def lane():
    return lax.broadcasted_iota(jnp.int32, (8, 128), 1)


def fill_weights(weights):
    a = lax.broadcasted_iota(jnp.int32, (128, 128), 0)
    b = lax.broadcasted_iota(jnp.int32, (128, 128), 1)
    ga, gb, za, zb = a // NZ, b // NZ, a % NZ, b % NZ
    for slot in range(4):
        if slot == 3:
            offset = jnp.where(ga == gb, (za - zb + 3 + NZ) % NZ, NZ)
        else:
            offset = jnp.where(za == zb, 4 * (slot - 1) + ga - gb + 3, NZ)
        for side, coefficients in enumerate((LOW, HIGH)):
            w = jnp.zeros((128, 128), jnp.float32)
            for m, c in enumerate(coefficients):
                if c:
                    w = jnp.where(offset == m, c, w)
            w = w.astype(jnp.bfloat16)
            weights[slot, 0:128, 128 * side : 128 * side + 128] = w
            weights[slot, 128:256, 128 * side : 128 * side + 128] = w


def split_tile(q, qb, t, row, blocks):
    size = 8 * blocks
    x = q[:, t, row : row + size, :].reshape(NV * size, 128) * (1.0 / 60.0)
    top = x.astype(jnp.bfloat16)
    qb[t, 0 : NV * size, 0:128] = top
    qb[t, 0 : NV * size, 128:256] = (x - top.astype(jnp.float32)).astype(jnp.bfloat16)


def dot(a, b):
    return jnp.dot(a, b, preferred_element_type=jnp.float32)


def store_primitives(q, t, row, c):
    for v, value in enumerate(primitives(c)):
        q[v, t, row : row + 8, :] = value


def inner_terms(q, qb, fs, fx, s, weights, rate, row=ROW0, blocks=2):
    pre, act, heat = rate
    size = 8 * blocks
    for t in (1, 2):
        split_tile(q, qb, t, row, blocks)
        fs[t - 1, 0 : NV * size] = dot(qb[t, 0 : NV * size], weights[3])
    first = lane() % NZ == NZ - 1

    def half(h, _):
        for kt in range(2):
            stencil = [
                [q[v, h + 1, row - 3 + 8 * kt + m : row + 5 + 8 * kt + m, :] for m in range(6)] for v in range(NV)
            ]
            pairs = [stencil_pair(x) for x in stencil]
            for v, f in enumerate(face_flux(lambda v: pairs[v][0], lambda v: pairs[v][1], 0)):
                fx[v, h, 8 * kt : 8 * kt + 8, :] = f
        for kt in range(blocks):
            rows = slice(8 * kt, 8 * kt + 8)
            cells = slice(row + 8 * kt, row + 8 * kt + 8)
            rho, pressure = q[0, h + 1, cells, :], q[4, h + 1, cells, :]
            ratio = rho / pressure
            rates = [
                pre[r] * rho * q[5 + r, h + 1, cells, :] * jnp.exp(-act[r] * ratio) for r in range(NR)
            ]
            release = heat[0] * rates[0]
            for r in range(1, NR):
                release = release + heat[r] * rates[r]
            source = [None] * 4 + [release, -rates[0]]
            source += [rates[r - 1] - rates[r] for r in range(1, NR)] + [rates[NR - 1]]
            flux = face_flux(
                lambda v: fs[h, size * v + 8 * kt : size * v + 8 * kt + 8, 0:128],
                lambda v: fs[h, size * v + 8 * kt : size * v + 8 * kt + 8, 128:256],
                2,
            )
            for v, f in enumerate(flux):
                above = jnp.where(first, pltpu.roll(f, NZ - 1, 1), pltpu.roll(f, 127, 1))
                x = (f - above) + (fx[v, h, rows, :] - fx[v, h, 8 * kt + 1 : 8 * kt + 9, :])
                if source[v] is not None:
                    x = x + source[v]
                s[v, h, rows, :] = x
        return 0

    lax.fori_loop(0, 2, half, 0)


def row_terms(q, qb, fs, fy, weights, row=ROW0, blocks=2):
    size = 8 * blocks
    split_tile(q, qb, 0, row, blocks)
    split_tile(q, qb, 3, row, blocks)
    tiles = [qb[t, 0 : NV * size] for t in range(4)]
    for j in range(3):
        x = dot(tiles[j], weights[0]) + dot(tiles[j + 1], weights[1])
        if j < 2:
            x = x + dot(tiles[j + 2], weights[2])
        fs[j, 0 : NV * size] = x

    def tile(j, _):
        for kt in range(blocks):
            flux = face_flux(
                lambda v: fs[j, size * v + 8 * kt : size * v + 8 * kt + 8, 0:128],
                lambda v: fs[j, size * v + 8 * kt : size * v + 8 * kt + 8, 128:256],
                1,
            )
            for v, f in enumerate(flux):
                fy[v, j, 8 * kt : 8 * kt + 8, :] = f
        return 0

    lax.fori_loop(0, 3, tile, 0)


def rate_of(s, fy, v, h, kt):
    rows = slice(8 * kt, 8 * kt + 8)
    f = fy[v, h, rows, :]
    last = lane() >= 96
    above = jnp.where(last, pltpu.roll(fy[v, h + 1, rows, :], 96, 1), pltpu.roll(f, 96, 1))
    return s[v, h, rows, :] + (f - above)


def mirrored(x, sign):
    group = lane() // NZ
    return sign * jnp.where(group % 2 == 0, pltpu.roll(x, 32, 1), pltpu.roll(x, 96, 1))


def pack(src, start, quarter, dst, to, free):
    group = lax.broadcasted_iota(jnp.int32, (quarter, 128), 1) // NZ
    last = src(start + 3 * quarter, quarter)
    for j in range(3):
        moved = pltpu.roll(last, (32 * (3 - j) if free == 3 else 128 - 32 * (j + 1)), 1)
        dst[to + j * quarter : to + (j + 1) * quarter, :] = jnp.where(
            group == free, moved, src(start + j * quarter, quarter)
        )


def unpack(src, start, quarter, dst, to, free):
    group = lax.broadcasted_iota(jnp.int32, (quarter, 128), 1) // NZ
    last = jnp.ones((quarter, 128), jnp.float32)
    for j in range(3):
        x = src[start + j * quarter : start + (j + 1) * quarter, :]
        dst[to + j * quarter : to + (j + 1) * quarter, :] = jnp.where(group == free, 1.0, x)
        last = jnp.where(group == (j if free == 3 else j + 1), pltpu.roll(x, 32 * (j + 1), 1), last)
    dst[to + 3 * quarter : to + 4 * quarter, :] = last


def kernel(n_gx, n_gy, u, fresh_in, slide, cuts_in, pre_in, act_in, heat_in, out, us, fresh, cuts, pre, act, heat, xw, yl, yh, fb, yf, xe, vw, xs, xl, xg, yl2, yh2, ps, yp, ps2, yp2,
           q, qb, fs, fx, fy, s, weights, send_sem, recv_sem, load_sem, late_sem):
    gx, gy = lax.axis_index("gx"), lax.axis_index("gy")
    has_prev, has_next = gx > 0, gx < n_gx - 1
    starts_run = jnp.logical_and(has_prev, lax.rem(gx, RUN) == 0)
    ends_run = jnp.logical_and(has_next, lax.rem(gx, RUN) == RUN - 1)
    has_below, has_above = gy > 0, gy < n_gy - 1
    inside = {-1: has_prev, 1: has_next}
    beside = {-1: has_below, 1: has_above}
    pairs = ((u, us), (fresh_in, fresh), (cuts_in, cuts), (pre_in, pre), (act_in, act), (heat_in, heat))
    loads = [pltpu.make_async_copy(a, b, load_sem.at[k]) for k, (a, b) in enumerate(pairs)]

    def both(a, b):
        return jnp.logical_and(a, b)

    goes_on, went_on = both(has_next, jnp.logical_not(ends_run)), both(has_prev, jnp.logical_not(starts_run))
    neighbours = [(a, b) for a in (-1, 0, 1) for b in (-1, 0, 1) if a or b]
    barrier = pltpu.get_barrier_semaphore()
    for dx, dy in neighbours:
        there = goes_on if dx == 1 else has_prev
        if dx and dy:
            there = both(there, beside[dy])
        elif dy:
            there = beside[dy]

        @pl.when(there)
        def _(dx=dx, dy=dy):
            pl.semaphore_signal(barrier, inc=1, device_id=(gx + dx, gy + dy), device_id_type=MESH)

    for load in loads:
        load.start()
    loads[0].wait()
    for p in range(PX):
        for h in range(2):
            xw[h, OWN + NV * p : OWN + NV * (p + 1), :] = us[p, :, 128 * h : 128 * h + 128]
    along = 1 + jnp.where(went_on, 1, 0) + jnp.where(has_next, 1, 0)
    across = 1 + jnp.where(has_below, 1, 0) + jnp.where(has_above, 1, 0)
    pl.semaphore_wait(barrier, along * across - 1)
    for dy in (-1, 0, 1):

        @pl.when(both(ends_run, beside[dy]) if dy else ends_run)
        def _(dy=dy):
            pl.semaphore_signal(late_sem, inc=1, device_id=(gx + 1, gy + dy), device_id_type=MESH)


    def remote(k, src, dst, dx, dy):
        return pltpu.make_async_remote_copy(
            src_ref=src, dst_ref=dst, send_sem=send_sem.at[k], recv_sem=recv_sem.at[k],
            device_id=(gx + dx, gy + dy), device_id_type=MESH,
        )

    x_first = [
        (has_next, remote(1, xw.at[:, OWN + 96 : NEXT], xw.at[:, OWN - 72 : OWN], 1, 0), has_prev),
    ]
    x_back = [(has_prev, remote(0, xw.at[:, OWN:NEXT], xw.at[:, NEXT : NEXT + PX * NV], -1, 0), has_next)]
    y_first, y_back = [], []
    lower = [(ends_run, remote(18, xw.at[:, OWN + 56 : OWN + 96], xe, 1, 0), starts_run)]
    for k, dy in enumerate((1, -1)):
        to, of = beside[dy], beside[-dy]
        for number, (go, come, dx, a, b) in enumerate((
            (ends_run, starts_run, 1, 248, 304),
            (has_prev, has_next, -1, 128, 224),
            (has_next, has_prev, 1, 224, 248),
        )):
            copy = remote(2 + 5 * k + number, ps.at[k, a:b], yp.at[k, a:b], dx, dy)
            (lower if a == 248 else y_back if dx < 0 else y_first).append((both(to, go), copy, both(of, come)))
        y_first.append((to, remote(5 + 5 * k, ps.at[k, 0:128], yp.at[k, 0:128], 0, dy), of))
        y_first.append((
            both(to, jnp.logical_not(has_next)),
            remote(6 + 5 * k, fb.at[1 - k], yf.at[k], 0, dy),
            both(of, jnp.logical_not(has_next)),
        ))

    def start(copies, now=True):
        for to, copy, _ in copies:

            @pl.when(both(to, now))
            def _(copy=copy):
                copy.start()

    def arrive(copies):
        for _, copy, of in copies:

            @pl.when(of)
            def _(copy=copy):
                copy.wait_recv()

    def leave(copies):
        for to, copy, _ in copies:

            @pl.when(to)
            def _(copy=copy):
                copy.wait_send()

    start(x_first)
    start(x_back, went_on)
    for k, h in ((0, 1), (1, 0)):
        for row, quarter, to in PARTS:
            pack(lambda a, n, h=h: xw[h, a : a + n, :], OWN + row, quarter, ps.at[k], to, 3 * k)

    for load in loads[1:]:
        load.wait()
    for h in range(2):
        fb[h, 0:NV, :] = fresh[:, 128 * h : 128 * h + 128]
        fb[h, NV:16, :] = jnp.zeros((2, 128), jnp.float32)
    start(y_back, went_on)
    start(y_first)

    @pl.when(ends_run)
    def _():
        row, quarter, to = RUN_PART
        for k, h in ((0, 1), (1, 0)):
            pack(lambda a, n, h=h: xw[h, a : a + n, :], OWN + row, quarter, ps.at[k], to, 3 * k)

    start(lower)
    base = jnp.clip(cuts[gx] - gx * PX + slide[0], -2, 9)
    count = jnp.clip(cuts[gx + 1] - cuts[gx], 9, CAP)
    fill_weights(weights)
    row_id = lax.broadcasted_iota(jnp.int32, (8, 128), 0)

    @pl.when(starts_run)
    def _():
        pl.semaphore_wait(late_sem, across)

    start(x_back, starts_run)
    start(y_back, starts_run)
    arrive(x_back)
    arrive(x_first)

    @pl.when(jnp.logical_not(has_next))
    def _():
        for p in range(12, 27):
            for h in range(2):
                xw[h, OWN + NV * p : OWN + NV * (p + 1), :] = fb[h, 0:NV, :]

    def window(h, k, v):
        return xw[h, pl.ds((base + ORIGIN + k) * NV + v, 8, stride=NV), :]

    low_edge = both(jnp.logical_not(has_prev), row_id < 3)

    def window_tile(h, _):
        for j in range(3):
            c = [window(h, 8 * j - 3, v) for v in range(NV)]
            if j == 0:
                c = [jnp.where(low_edge, xw[h, pl.ds((base + ORIGIN) * NV + v, 1), :], c[v]) for v in range(NV)]
            store_primitives(q, h + 1, 8 * j + 8, c)
        return 0

    lax.fori_loop(0, 2, window_tile, 0)
    inner_terms(q, qb, fs, fx, s, weights, (pre, act, heat))

    arrive(y_back)
    arrive(y_first)
    for k, ghost in ((0, yl), (1, yh)):
        for (_, quarter, row), to in zip(PARTS, (Y_OWN, Y_NEXT, Y_OWN - 32)):
            unpack(yp.at[k], row, quarter, ghost, to, 3 * k)

    @pl.when(jnp.logical_not(has_next))
    def _():
        for p in range(12, 21):
            for ghost, k in ((yl, 0), (yh, 1)):
                ghost[Y_OWN + NV * p : Y_OWN + NV * (p + 1), :] = yf[k, 0:NV, :]

    def beside_tiles(k):
        for t, h, ghost, is_wall in ((0, 0, yl, jnp.logical_not(has_below)), (3, 1, yh, jnp.logical_not(has_above))):

            @pl.when(is_wall)
            def _(t=t, h=h):
                c = [mirrored(window(h, k, v), -1.0 if v == 2 else 1.0) for v in range(NV)]
                store_primitives(q, t, ROW0 + k, c)

            @pl.when(jnp.logical_not(is_wall))
            def _(t=t, ghost=ghost):
                c = [ghost[pl.ds((base + Y_ORIGIN + k) * NV + v, 8, stride=NV), :] for v in range(NV)]
                store_primitives(q, t, ROW0 + k, c)

    for k in (0, 8):
        beside_tiles(k)

    row_terms(q, qb, fs, fy, weights)

    def first_update(h, _):
        for kt in range(2):
            for v in range(NV):
                x = window(h, 8 * kt, v) + TIME_STEP * rate_of(s, fy, v, h, kt)
                vw[h, pl.ds(V_OWN + 8 * kt * NV + v, 8, stride=NV), :] = x
        return 0

    lax.fori_loop(0, 2, first_update, 0)

    for h in range(2):
        xs[h] = vw[h, pl.ds(V_OWN + (count - 3) * NV - 6, 48), :]
    second = [
        (has_prev, remote(12, vw.at[:, V_OWN : V_OWN + 48], xg.at[:, G_OWN : G_OWN + 48], -1, 0), has_next),
        (goes_on, remote(13, xs, xl.at[:, 0:48], 1, 0), went_on),
    ]
    y_second = [
        (has_above, remote(14, ps2.at[0], yp2.at[0], 0, 1), has_below),
        (has_below, remote(15, ps2.at[1], yp2.at[1], 0, -1), has_above),
    ]
    start(second)
    for k, h in ((0, 1), (1, 0)):
        pack(lambda a, n, h=h: vw[h, a : a + n, :], V_OWN, 56, ps2.at[k], 0, 3 * k)
    start(y_second)

    @pl.when(jnp.logical_not(has_next))
    def _():
        for p in range(3):
            for h in range(2):
                xg[h, G_OWN + NV * p : G_OWN + NV * (p + 1), :] = fb[h, 0:NV, :]

    arrive(lower)

    @pl.when(starts_run)
    def _():
        for h in range(2):
            xw[h, OWN - 112 : OWN - 72, :] = xe[h]
        for k, ghost in ((0, yl), (1, yh)):
            unpack(yp.at[k], RUN_PART[2], RUN_PART[1], ghost, Y_OWN - 72, 3 * k)

        def lower_tile(h, _):
            store_primitives(q, h + 1, 0, [window(h, -ROW0, v) for v in range(NV)])
            return 0

        lax.fori_loop(0, 2, lower_tile, 0)
        beside_tiles(-8)
        inner_terms(q, qb, fs, fx, s, weights, (pre, act, heat), ROW0 - 8, 1)
        row_terms(q, qb, fs, fy, weights, ROW0 - 8, 1)

        def lower_update(h, _):
            for v in range(NV):
                x = window(h, -8, v) + TIME_STEP * rate_of(s, fy, v, h, 0)
                xl[h, pl.ds(6 + v, 3, stride=NV), :] = x[5:8]
            return 0

        lax.fori_loop(0, 2, lower_update, 0)

    arrive(second)

    def second_tile(h, _):
        for j in range(3):
            k = 8 * j - 3
            c = [vw[h, pl.ds(V_OWN + k * NV + v, 8, stride=NV), :] for v in range(NV)]
            if j == 0:
                ghosts = [xl[h, pl.ds(6 + v, 8, stride=NV), :] for v in range(NV)]
                c = [jnp.where(row_id < 3, ghosts[v], c[v]) for v in range(NV)]
                c = [jnp.where(low_edge, vw[h, V_OWN + v : V_OWN + v + 1, :], c[v]) for v in range(NV)]
            else:
                owned = row_id + k < count
                c = [
                    jnp.where(owned, c[v], xg[h, pl.ds(G_OWN + (k - count) * NV + v, 8, stride=NV), :])
                    for v in range(NV)
                ]
            store_primitives(q, h + 1, 8 * j + 8, c)
        return 0

    lax.fori_loop(0, 2, second_tile, 0)
    inner_terms(q, qb, fs, fx, s, weights, (pre, act, heat))

    arrive(y_second)
    for k, ghost in ((0, yl2), (1, yh2)):
        unpack(yp2.at[k], 0, 56, ghost, 0, 3 * k)
    for t, h, ghost, is_wall in ((0, 0, yl2, jnp.logical_not(has_below)), (3, 1, yh2, jnp.logical_not(has_above))):
        for kt in range(2):

            @pl.when(is_wall)
            def _(t=t, h=h, kt=kt):
                c = [
                    mirrored(vw[h, pl.ds(V_OWN + 8 * kt * NV + v, 8, stride=NV), :], -1.0 if v == 2 else 1.0)
                    for v in range(NV)
                ]
                store_primitives(q, t, ROW0 + 8 * kt, c)

            @pl.when(jnp.logical_not(is_wall))
            def _(t=t, ghost=ghost, kt=kt):
                c = [ghost[pl.ds(8 * kt * NV + v, 8, stride=NV), :] for v in range(NV)]
                store_primitives(q, t, ROW0 + 8 * kt, c)

    row_terms(q, qb, fs, fy, weights)
    for h in range(2):
        for kt in range(2):
            owned = row_id + 8 * kt < count
            for v in range(NV):
                w = window(h, 8 * kt, v)
                x = vw[h, pl.ds(V_OWN + 8 * kt * NV + v, 8, stride=NV), :] + TIME_STEP * rate_of(s, fy, v, h, kt)
                x = jnp.where(owned, 0.75 * w + 0.25 * x, 0.0)
                if kt == 0:
                    out[v, 0:8, 128 * h : 128 * h + 128] = x
                else:
                    out[v, 8:CAP, 128 * h : 128 * h + 128] = x[0 : CAP - 8]

    leave(lower)
    leave(x_back)
    leave(y_back)
    leave(x_first)
    leave(y_first)
    leave(second)
    leave(y_second)


def body(n_gx, n_gy, gas_state, inflow, slide_count, cut_list, prefactor, activation, heat_release):
    def f32(*shape):
        return pltpu.VMEM(shape, jnp.float32)

    return pl.pallas_call(
        functools.partial(kernel, n_gx, n_gy),
        out_shape=pltpu.VMEM((NV, CAP, 256), jnp.float32),
        in_specs=[pl.BlockSpec(memory_space=m) for m in [pltpu.HBM] * 2 + [pltpu.SMEM] + [pltpu.HBM] * 4],
        out_specs=pl.BlockSpec(memory_space=pltpu.VMEM),
        scratch_shapes=[
            f32(PX, NV, 256),
            f32(NV, 256),
            pltpu.SMEM((n_gx + 1,), jnp.int32),
            pltpu.SMEM((NR,), jnp.float32),
            pltpu.SMEM((NR,), jnp.float32),
            pltpu.SMEM((NR,), jnp.float32),
            f32(2, W_ROWS, 128),
            f32(Y_ROWS, 128),
            f32(Y_ROWS, 128),
            f32(2, 16, 128),
            f32(2, 16, 128),
            f32(2, 40, 128),
            f32(2, V_ROWS, 128),
            f32(2, 48, 128),
            f32(2, 136, 128),
            f32(2, G_ROWS, 128),
            f32(240, 128),
            f32(240, 128),
            f32(2, 304, 128),
            f32(2, 304, 128),
            f32(2, 168, 128),
            f32(2, 168, 128),
            f32(NV, 4, 32, 128),
            pltpu.VMEM((4, NV * 16, 256), jnp.bfloat16),
            f32(3, NV * 16, 256),
            f32(NV, 2, 24, 128),
            f32(NV, 3, 16, 128),
            f32(NV, 2, 16, 128),
            pltpu.VMEM((4, 256, 256), jnp.bfloat16),
            pltpu.SemaphoreType.DMA((19,)),
            pltpu.SemaphoreType.DMA((19,)),
            pltpu.SemaphoreType.DMA((6,)),
            pltpu.SemaphoreType.REGULAR,
        ],
        compiler_params=pltpu.CompilerParams(
            collective_id=0, has_side_effects=True, vmem_limit_bytes=32 * 1024 * 1024
        ),
        name="two_stages",
    )(*[
        x if x is slide_count else pltpu.with_memory_space_constraint(x, pltpu.HBM)
        for x in (
            jnp.transpose(gas_state, (1, 0, 2)), inflow, slide_count, cut_list, prefactor, activation, heat_release
        )
    ])


def solution(mesh):
    in_specs = (P(None, "gx", "gy"), P(None, "gy"), P(), P(), P(), P(), P())
    return jax.shard_map(
        functools.partial(body, mesh.shape["gx"], mesh.shape["gy"]),
        mesh=mesh,
        in_specs=in_specs,
        out_specs=P(None, "gx", "gy"),
        check_vma=False,
    )
```

```python
import functools

import jax
import jax.numpy as jnp
from jax import lax
from jax.experimental import pallas as pl
from jax.experimental.pallas import tpu as pltpu
from jax.sharding import PartitionSpec as P

MESH = pl.DeviceIdType.MESH
NV = 14
NR = 8
PX = 12
CAP = 15
NZ = 32
GAS_GAMMA = 1.4
TIME_STEP = 0.025

ORIGIN = 16
OWN = ORIGIN * NV
NEXT = OWN + PX * NV
Y_ORIGIN = 12
Y_OWN = Y_ORIGIN * NV
Y_NEXT = Y_OWN + PX * NV
V_OWN = 4 * NV
G_OWN = 12 * NV

PARTS = ((0, 42, 0), (0, 32, 128), (136, 8, 224))
RUN_PART = (96, 11, 248)
RUN = 32
ROW0 = 11

W_ROWS = 672
Y_ROWS = 544
V_ROWS = 56 + 24 * NV
G_ROWS = 352

LOW = (2.0, -13.0, 47.0, 27.0, -3.0, 0.0)
HIGH = (0.0, -3.0, 27.0, 47.0, -13.0, 2.0)


def stencil_pair(q):
    d = [c / 60.0 for c in (2.0, 13.0, 47.0, 27.0, 3.0)]
    low = (d[0] * q[0] - d[1] * q[1]) + (d[2] * q[2] + d[3] * q[3]) - d[4] * q[4]
    high = (d[3] * q[2] - d[4] * q[1]) + (d[2] * q[3] - d[1] * q[4]) + d[0] * q[5]
    return low, high


def wave_speed(normal, pressure, density):
    scaled = GAS_GAMMA * pressure
    return jnp.abs(normal) + jnp.abs(scaled) * lax.rsqrt(jnp.maximum(scaled * density, 1e-30))


def face_flux(low, high, direction):
    rho_l, rho_r, p_l, p_r = low(0), high(0), low(4), high(4)
    u_l = [low(1 + j) for j in range(3)]
    u_r = [high(1 + j) for j in range(3)]
    n_l, n_r = u_l[direction], u_r[direction]
    speed = jnp.maximum(wave_speed(n_l, p_l, rho_l), wave_speed(n_r, p_r, rho_r))
    a_l, a_r = 0.5 * (n_l + speed), 0.5 * (n_r - speed)
    m_l, m_r = rho_l * a_l, rho_r * a_r
    flux = [m_l + m_r]
    for j in range(3):
        f = m_l * u_l[j] + m_r * u_r[j]
        if j == direction:
            f = f + 0.5 * (p_l + p_r)
        flux.append(f)
    k_l = u_l[0] * u_l[0] + u_l[1] * u_l[1] + u_l[2] * u_l[2]
    k_r = u_r[0] * u_r[0] + u_r[1] * u_r[1] + u_r[2] * u_r[2]
    flux.append(
        p_l * (2.5 * a_l + 0.5 * n_l) + p_r * (2.5 * a_r + 0.5 * n_r) + 0.5 * (m_l * k_l + m_r * k_r)
    )
    for j in range(5, NV):
        flux.append(m_l * low(j) + m_r * high(j))
    return flux


def primitives(c):
    inverse = 1.0 / c[0]
    u = [c[j] * inverse for j in (1, 2, 3)]
    kinetic = 0.5 * (c[1] * u[0] + c[2] * u[1] + c[3] * u[2])
    return [c[0]] + u + [0.4 * (c[4] - kinetic)] + [c[j] * inverse for j in range(5, NV)]


def lane():
    return lax.broadcasted_iota(jnp.int32, (8, 128), 1)


def fill_weights(weights):
    a = lax.broadcasted_iota(jnp.int32, (128, 128), 0)
    b = lax.broadcasted_iota(jnp.int32, (128, 128), 1)
    ga, gb, za, zb = a // NZ, b // NZ, a % NZ, b % NZ
    for slot in range(4):
        if slot == 3:
            offset = jnp.where(ga == gb, (za - zb + 3 + NZ) % NZ, NZ)
        else:
            offset = jnp.where(za == zb, 4 * (slot - 1) + ga - gb + 3, NZ)
        for side, coefficients in enumerate((LOW, HIGH)):
            w = jnp.zeros((128, 128), jnp.float32)
            for m, c in enumerate(coefficients):
                if c:
                    w = jnp.where(offset == m, c, w)
            w = w.astype(jnp.bfloat16)
            weights[slot, 0:128, 128 * side : 128 * side + 128] = w
            weights[slot, 128:256, 128 * side : 128 * side + 128] = w


def split_tile(q, qb, t, row, blocks):
    size = 8 * blocks
    x = q[:, t, row : row + size, :].reshape(NV * size, 128) * (1.0 / 60.0)
    top = x.astype(jnp.bfloat16)
    qb[t, 0 : NV * size, 0:128] = top
    qb[t, 0 : NV * size, 128:256] = (x - top.astype(jnp.float32)).astype(jnp.bfloat16)


def dot(a, b):
    return jnp.dot(a, b, preferred_element_type=jnp.float32)


def store_primitives(q, t, row, c):
    for v, value in enumerate(primitives(c)):
        q[v, t, row : row + 8, :] = value


def inner_terms(q, qb, fs, fx, s, weights, rate, row=ROW0, blocks=2):
    pre, act, heat = rate
    size = 8 * blocks
    for t in (1, 2):
        split_tile(q, qb, t, row, blocks)
    x, y = qb[1, 0 : NV * size], qb[2, 0 : NV * size]
    fs[0, 0 : NV * size] = dot(x, weights[3])
    fs[1, 0 : NV * size] = dot(y, weights[3])
    fs[2, 0 : NV * size] = dot(x, weights[1]) + dot(y, weights[2])
    fs[3, 0 : NV * size] = dot(x, weights[0]) + dot(y, weights[1])
    fs[4, 0 : NV * size] = dot(y, weights[0])
    first = lane() % NZ == NZ - 1

    def half(h, _):
        for kt in range(2):
            stencil = [
                [q[v, h + 1, row - 3 + 8 * kt + m : row + 5 + 8 * kt + m, :] for m in range(6)] for v in range(NV)
            ]
            pairs = [stencil_pair(x) for x in stencil]
            for v, f in enumerate(face_flux(lambda v: pairs[v][0], lambda v: pairs[v][1], 0)):
                fx[v, h, 8 * kt : 8 * kt + 8, :] = f
        for kt in range(blocks):
            rows = slice(8 * kt, 8 * kt + 8)
            cells = slice(row + 8 * kt, row + 8 * kt + 8)
            rho, pressure = q[0, h + 1, cells, :], q[4, h + 1, cells, :]
            ratio = rho / pressure
            rates = [
                pre[r] * rho * q[5 + r, h + 1, cells, :] * jnp.exp(-act[r] * ratio) for r in range(NR)
            ]
            release = heat[0] * rates[0]
            for r in range(1, NR):
                release = release + heat[r] * rates[r]
            source = [None] * 4 + [release, -rates[0]]
            source += [rates[r - 1] - rates[r] for r in range(1, NR)] + [rates[NR - 1]]
            flux = face_flux(
                lambda v: fs[h, size * v + 8 * kt : size * v + 8 * kt + 8, 0:128],
                lambda v: fs[h, size * v + 8 * kt : size * v + 8 * kt + 8, 128:256],
                2,
            )
            for v, f in enumerate(flux):
                above = jnp.where(first, pltpu.roll(f, NZ - 1, 1), pltpu.roll(f, 127, 1))
                x = (f - above) + (fx[v, h, rows, :] - fx[v, h, 8 * kt + 1 : 8 * kt + 9, :])
                if source[v] is not None:
                    x = x + source[v]
                s[v, h, rows, :] = x
        return 0

    lax.fori_loop(0, 2, half, 0)


def row_terms(q, qb, fs, fy, weights, row=ROW0, blocks=2):
    size = 8 * blocks
    split_tile(q, qb, 0, row, blocks)
    split_tile(q, qb, 3, row, blocks)
    x, y = qb[0, 0 : NV * size], qb[3, 0 : NV * size]
    fs[2, 0 : NV * size] += dot(x, weights[0])
    fs[3, 0 : NV * size] += dot(y, weights[2])
    fs[4, 0 : NV * size] += dot(y, weights[1])

    def tile(j, _):
        for kt in range(blocks):
            flux = face_flux(
                lambda v: fs[j + 2, size * v + 8 * kt : size * v + 8 * kt + 8, 0:128],
                lambda v: fs[j + 2, size * v + 8 * kt : size * v + 8 * kt + 8, 128:256],
                1,
            )
            for v, f in enumerate(flux):
                fy[v, j, 8 * kt : 8 * kt + 8, :] = f
        return 0

    lax.fori_loop(0, 3, tile, 0)


def rate_of(s, fy, v, h, kt):
    rows = slice(8 * kt, 8 * kt + 8)
    f = fy[v, h, rows, :]
    last = lane() >= 96
    above = jnp.where(last, pltpu.roll(fy[v, h + 1, rows, :], 96, 1), pltpu.roll(f, 96, 1))
    return s[v, h, rows, :] + (f - above)


def mirrored(x, sign):
    group = lane() // NZ
    return sign * jnp.where(group % 2 == 0, pltpu.roll(x, 32, 1), pltpu.roll(x, 96, 1))


def pack(src, start, quarter, dst, to, free):
    group = lax.broadcasted_iota(jnp.int32, (quarter, 128), 1) // NZ
    last = src(start + 3 * quarter, quarter)
    for j in range(3):
        moved = pltpu.roll(last, (32 * (3 - j) if free == 3 else 128 - 32 * (j + 1)), 1)
        dst[to + j * quarter : to + (j + 1) * quarter, :] = jnp.where(
            group == free, moved, src(start + j * quarter, quarter)
        )


def unpack(src, start, quarter, dst, to, free):
    group = lax.broadcasted_iota(jnp.int32, (quarter, 128), 1) // NZ
    last = jnp.ones((quarter, 128), jnp.float32)
    for j in range(3):
        x = src[start + j * quarter : start + (j + 1) * quarter, :]
        dst[to + j * quarter : to + (j + 1) * quarter, :] = jnp.where(group == free, 1.0, x)
        last = jnp.where(group == (j if free == 3 else j + 1), pltpu.roll(x, 32 * (j + 1), 1), last)
    dst[to + 3 * quarter : to + 4 * quarter, :] = last


def kernel(n_gx, n_gy, u, fresh_in, slide, cuts_in, pre_in, act_in, heat_in, out, us, fresh, cuts, pre, act, heat, xw, yl, yh, fb, yf, xe, vw, xs, xl, xg, yl2, yh2, ps, yp, ps2, yp2,
           q, qb, fs, fx, fy, s, weights, send_sem, recv_sem, load_sem, late_sem):
    gx, gy = lax.axis_index("gx"), lax.axis_index("gy")
    has_prev, has_next = gx > 0, gx < n_gx - 1
    starts_run = jnp.logical_and(has_prev, lax.rem(gx, RUN) == 0)
    ends_run = jnp.logical_and(has_next, lax.rem(gx, RUN) == RUN - 1)
    has_below, has_above = gy > 0, gy < n_gy - 1
    inside = {-1: has_prev, 1: has_next}
    beside = {-1: has_below, 1: has_above}
    pairs = ((u, us), (fresh_in, fresh), (cuts_in, cuts), (pre_in, pre), (act_in, act), (heat_in, heat))
    loads = [pltpu.make_async_copy(a, b, load_sem.at[k]) for k, (a, b) in enumerate(pairs)]

    def both(a, b):
        return jnp.logical_and(a, b)

    goes_on, went_on = both(has_next, jnp.logical_not(ends_run)), both(has_prev, jnp.logical_not(starts_run))
    neighbours = [(a, b) for a in (-1, 0, 1) for b in (-1, 0, 1) if a or b]
    barrier = pltpu.get_barrier_semaphore()
    for dx, dy in neighbours:
        there = goes_on if dx == 1 else has_prev
        if dx and dy:
            there = both(there, beside[dy])
        elif dy:
            there = beside[dy]

        @pl.when(there)
        def _(dx=dx, dy=dy):
            pl.semaphore_signal(barrier, inc=1, device_id=(gx + dx, gy + dy), device_id_type=MESH)

    for load in loads:
        load.start()
    loads[0].wait()
    for p in range(PX):
        for h in range(2):
            xw[h, OWN + NV * p : OWN + NV * (p + 1), :] = us[p, :, 128 * h : 128 * h + 128]
    along = 1 + jnp.where(went_on, 1, 0) + jnp.where(has_next, 1, 0)
    across = 1 + jnp.where(has_below, 1, 0) + jnp.where(has_above, 1, 0)
    pl.semaphore_wait(barrier, along * across - 1)
    for dy in (-1, 0, 1):

        @pl.when(both(ends_run, beside[dy]) if dy else ends_run)
        def _(dy=dy):
            pl.semaphore_signal(late_sem, inc=1, device_id=(gx + 1, gy + dy), device_id_type=MESH)


    def remote(k, src, dst, dx, dy):
        return pltpu.make_async_remote_copy(
            src_ref=src, dst_ref=dst, send_sem=send_sem.at[k], recv_sem=recv_sem.at[k],
            device_id=(gx + dx, gy + dy), device_id_type=MESH,
        )

    x_first = [
        (has_next, remote(1, xw.at[:, OWN + 96 : NEXT], xw.at[:, OWN - 72 : OWN], 1, 0), has_prev),
    ]
    x_back = [(has_prev, remote(0, xw.at[:, OWN:NEXT], xw.at[:, NEXT : NEXT + PX * NV], -1, 0), has_next)]
    y_first, y_back, y_near = [], [], []
    lower = [(ends_run, remote(18, xw.at[:, OWN + 56 : OWN + 96], xe, 1, 0), starts_run)]
    for k, dy in enumerate((1, -1)):
        to, of = beside[dy], beside[-dy]
        for number, (go, come, dx, a, b) in enumerate((
            (ends_run, starts_run, 1, 248, 288),
            (has_prev, has_next, -1, 128, 224),
            (has_next, has_prev, 1, 224, 248),
        )):
            copy = remote(2 + 5 * k + number, ps.at[k, a:b], yp.at[k, a:b], dx, dy)
            (lower if a == 248 else y_back if dx < 0 else y_near).append((both(to, go), copy, both(of, come)))
        y_first.append((to, remote(5 + 5 * k, ps.at[k, 0:128], yp.at[k, 0:128], 0, dy), of))
        y_first.append((
            both(to, jnp.logical_not(has_next)),
            remote(6 + 5 * k, fb.at[1 - k], yf.at[k], 0, dy),
            both(of, jnp.logical_not(has_next)),
        ))

    def start(copies, now=True):
        for to, copy, _ in copies:

            @pl.when(both(to, now))
            def _(copy=copy):
                copy.start()

    def arrive(copies):
        for _, copy, of in copies:

            @pl.when(of)
            def _(copy=copy):
                copy.wait_recv()

    def leave(copies):
        for to, copy, _ in copies:

            @pl.when(to)
            def _(copy=copy):
                copy.wait_send()

    def pack_part(part):
        row, quarter, to = part
        for k, h in ((0, 1), (1, 0)):
            pack(lambda a, n, h=h: xw[h, a : a + n, :], OWN + row, quarter, ps.at[k], to, 3 * k)

    start(x_first)
    pack_part(PARTS[2])
    start(y_near)
    start(lower[:1])

    @pl.when(ends_run)
    def _():
        pack_part(RUN_PART)

    start(lower[1:])
    pack_part(PARTS[1])
    start(y_back, went_on)
    pack_part(PARTS[0])
    for load in loads[1:]:
        load.wait()
    for h in range(2):
        fb[h, 0:NV, :] = fresh[:, 128 * h : 128 * h + 128]
        fb[h, NV:16, :] = jnp.zeros((2, 128), jnp.float32)
    start(y_first)
    start(x_back, went_on)
    base = jnp.clip(cuts[gx] - gx * PX + slide[0], -2, 9)
    count = jnp.clip(cuts[gx + 1] - cuts[gx], 9, CAP)
    fill_weights(weights)
    row_id = lax.broadcasted_iota(jnp.int32, (8, 128), 0)

    @pl.when(starts_run)
    def _():
        pl.semaphore_wait(late_sem, across)

    start(x_back, starts_run)
    start(y_back, starts_run)
    arrive(x_back)
    arrive(x_first)

    @pl.when(jnp.logical_not(has_next))
    def _():
        for p in range(12, 27):
            for h in range(2):
                xw[h, OWN + NV * p : OWN + NV * (p + 1), :] = fb[h, 0:NV, :]

    def window(h, k, v):
        return xw[h, pl.ds((base + ORIGIN + k) * NV + v, 8, stride=NV), :]

    low_edge = both(jnp.logical_not(has_prev), row_id < 3)

    def window_tile(h, _):
        for j in range(3):
            c = [window(h, 8 * j - 3, v) for v in range(NV)]
            if j == 0:
                c = [jnp.where(low_edge, xw[h, pl.ds((base + ORIGIN) * NV + v, 1), :], c[v]) for v in range(NV)]
            store_primitives(q, h + 1, 8 * j + 8, c)
        return 0

    lax.fori_loop(0, 2, window_tile, 0)
    inner_terms(q, qb, fs, fx, s, weights, (pre, act, heat))

    arrive(y_back)
    arrive(y_near)
    arrive(y_first)
    for k, ghost in ((0, yl), (1, yh)):
        for (_, quarter, row), to in zip(PARTS, (Y_OWN, Y_NEXT, Y_OWN - 32)):
            unpack(yp.at[k], row, quarter, ghost, to, 3 * k)

    @pl.when(jnp.logical_not(has_next))
    def _():
        for p in range(12, 21):
            for ghost, k in ((yl, 0), (yh, 1)):
                ghost[Y_OWN + NV * p : Y_OWN + NV * (p + 1), :] = yf[k, 0:NV, :]

    def beside_tiles(k):
        for t, h, ghost, is_wall in ((0, 0, yl, jnp.logical_not(has_below)), (3, 1, yh, jnp.logical_not(has_above))):

            @pl.when(is_wall)
            def _(t=t, h=h):
                c = [mirrored(window(h, k, v), -1.0 if v == 2 else 1.0) for v in range(NV)]
                store_primitives(q, t, ROW0 + k, c)

            @pl.when(jnp.logical_not(is_wall))
            def _(t=t, ghost=ghost):
                c = [ghost[pl.ds((base + Y_ORIGIN + k) * NV + v, 8, stride=NV), :] for v in range(NV)]
                store_primitives(q, t, ROW0 + k, c)

    for k in (0, 8):
        beside_tiles(k)

    row_terms(q, qb, fs, fy, weights)

    def first_update(h, _):
        for kt in range(2):
            for v in range(NV):
                x = window(h, 8 * kt, v) + TIME_STEP * rate_of(s, fy, v, h, kt)
                vw[h, pl.ds(V_OWN + 8 * kt * NV + v, 8, stride=NV), :] = x
        return 0

    lax.fori_loop(0, 2, first_update, 0)

    for h in range(2):
        xs[h] = vw[h, pl.ds(V_OWN + (count - 3) * NV - 6, 48), :]
    second = [
        (has_prev, remote(12, vw.at[:, V_OWN : V_OWN + 48], xg.at[:, G_OWN : G_OWN + 48], -1, 0), has_next),
        (goes_on, remote(13, xs, xl.at[:, 0:48], 1, 0), went_on),
    ]
    y_second = [
        (has_above, remote(14, ps2.at[0], yp2.at[0], 0, 1), has_below),
        (has_below, remote(15, ps2.at[1], yp2.at[1], 0, -1), has_above),
    ]
    start(second)
    for k, h in ((0, 1), (1, 0)):
        pack(lambda a, n, h=h: vw[h, a : a + n, :], V_OWN, 56, ps2.at[k], 0, 3 * k)
    start(y_second)

    @pl.when(jnp.logical_not(has_next))
    def _():
        for p in range(3):
            for h in range(2):
                xg[h, G_OWN + NV * p : G_OWN + NV * (p + 1), :] = fb[h, 0:NV, :]

    arrive(lower)

    @pl.when(starts_run)
    def _():
        for h in range(2):
            xw[h, OWN - 112 : OWN - 72, :] = xe[h]
        for k, ghost in ((0, yl), (1, yh)):
            unpack(yp.at[k], RUN_PART[2], RUN_PART[1], ghost, Y_OWN - 72, 3 * k)

        def lower_tile(h, _):
            store_primitives(q, h + 1, 0, [window(h, -ROW0, v) for v in range(NV)])
            return 0

        lax.fori_loop(0, 2, lower_tile, 0)
        beside_tiles(-8)
        inner_terms(q, qb, fs, fx, s, weights, (pre, act, heat), ROW0 - 8, 1)
        row_terms(q, qb, fs, fy, weights, ROW0 - 8, 1)

        def lower_update(h, _):
            for v in range(NV):
                x = window(h, -8, v) + TIME_STEP * rate_of(s, fy, v, h, 0)
                xl[h, pl.ds(6 + v, 3, stride=NV), :] = x[5:8]
            return 0

        lax.fori_loop(0, 2, lower_update, 0)

    arrive(second)

    def second_tile(h, _):
        for j in range(3):
            k = 8 * j - 3
            c = [vw[h, pl.ds(V_OWN + k * NV + v, 8, stride=NV), :] for v in range(NV)]
            if j == 0:
                ghosts = [xl[h, pl.ds(6 + v, 8, stride=NV), :] for v in range(NV)]
                c = [jnp.where(row_id < 3, ghosts[v], c[v]) for v in range(NV)]
                c = [jnp.where(low_edge, vw[h, V_OWN + v : V_OWN + v + 1, :], c[v]) for v in range(NV)]
            else:
                owned = row_id + k < count
                c = [
                    jnp.where(owned, c[v], xg[h, pl.ds(G_OWN + (k - count) * NV + v, 8, stride=NV), :])
                    for v in range(NV)
                ]
            store_primitives(q, h + 1, 8 * j + 8, c)
        return 0

    lax.fori_loop(0, 2, second_tile, 0)
    inner_terms(q, qb, fs, fx, s, weights, (pre, act, heat))

    arrive(y_second)
    for k, ghost in ((0, yl2), (1, yh2)):
        unpack(yp2.at[k], 0, 56, ghost, 0, 3 * k)
    for t, h, ghost, is_wall in ((0, 0, yl2, jnp.logical_not(has_below)), (3, 1, yh2, jnp.logical_not(has_above))):
        for kt in range(2):

            @pl.when(is_wall)
            def _(t=t, h=h, kt=kt):
                c = [
                    mirrored(vw[h, pl.ds(V_OWN + 8 * kt * NV + v, 8, stride=NV), :], -1.0 if v == 2 else 1.0)
                    for v in range(NV)
                ]
                store_primitives(q, t, ROW0 + 8 * kt, c)

            @pl.when(jnp.logical_not(is_wall))
            def _(t=t, ghost=ghost, kt=kt):
                c = [ghost[pl.ds(8 * kt * NV + v, 8, stride=NV), :] for v in range(NV)]
                store_primitives(q, t, ROW0 + 8 * kt, c)

    row_terms(q, qb, fs, fy, weights)
    for h in range(2):
        for kt in range(2):
            owned = row_id + 8 * kt < count
            for v in range(NV):
                w = window(h, 8 * kt, v)
                x = vw[h, pl.ds(V_OWN + 8 * kt * NV + v, 8, stride=NV), :] + TIME_STEP * rate_of(s, fy, v, h, kt)
                x = jnp.where(owned, 0.75 * w + 0.25 * x, 0.0)
                if kt == 0:
                    out[v, 0:8, 128 * h : 128 * h + 128] = x
                else:
                    out[v, 8:CAP, 128 * h : 128 * h + 128] = x[0 : CAP - 8]

    leave(lower)
    leave(x_back)
    leave(y_back)
    leave(x_first)
    leave(y_near)
    leave(y_first)
    leave(second)
    leave(y_second)


def body(n_gx, n_gy, gas_state, inflow, slide_count, cut_list, prefactor, activation, heat_release):
    def f32(*shape):
        return pltpu.VMEM(shape, jnp.float32)

    return pl.pallas_call(
        functools.partial(kernel, n_gx, n_gy),
        out_shape=pltpu.VMEM((NV, CAP, 256), jnp.float32),
        in_specs=[pl.BlockSpec(memory_space=m) for m in [pltpu.HBM] * 2 + [pltpu.SMEM] + [pltpu.HBM] * 4],
        out_specs=pl.BlockSpec(memory_space=pltpu.VMEM),
        scratch_shapes=[
            f32(PX, NV, 256),
            f32(NV, 256),
            pltpu.SMEM((n_gx + 1,), jnp.int32),
            pltpu.SMEM((NR,), jnp.float32),
            pltpu.SMEM((NR,), jnp.float32),
            pltpu.SMEM((NR,), jnp.float32),
            f32(2, W_ROWS, 128),
            f32(Y_ROWS, 128),
            f32(Y_ROWS, 128),
            f32(2, 16, 128),
            f32(2, 16, 128),
            f32(2, 40, 128),
            f32(2, V_ROWS, 128),
            f32(2, 48, 128),
            f32(2, 136, 128),
            f32(2, G_ROWS, 128),
            f32(240, 128),
            f32(240, 128),
            f32(2, 288, 128),
            f32(2, 288, 128),
            f32(2, 168, 128),
            f32(2, 168, 128),
            f32(NV, 4, 32, 128),
            pltpu.VMEM((4, NV * 16, 256), jnp.bfloat16),
            f32(5, NV * 16, 256),
            f32(NV, 2, 24, 128),
            f32(NV, 3, 16, 128),
            f32(NV, 2, 16, 128),
            pltpu.VMEM((4, 256, 256), jnp.bfloat16),
            pltpu.SemaphoreType.DMA((19,)),
            pltpu.SemaphoreType.DMA((19,)),
            pltpu.SemaphoreType.DMA((6,)),
            pltpu.SemaphoreType.REGULAR,
        ],
        compiler_params=pltpu.CompilerParams(
            collective_id=0, has_side_effects=True, vmem_limit_bytes=32 * 1024 * 1024
        ),
        name="two_stages",
    )(*[
        x if x is slide_count else pltpu.with_memory_space_constraint(x, pltpu.HBM)
        for x in (
            jnp.transpose(gas_state, (1, 0, 2)), inflow, slide_count, cut_list, prefactor, activation, heat_release
        )
    ])


def solution(mesh):
    in_specs = (P(None, "gx", "gy"), P(None, "gy"), P(), P(), P(), P(), P())
    return jax.shard_map(
        functools.partial(body, mesh.shape["gx"], mesh.shape["gy"]),
        mesh=mesh,
        in_specs=in_specs,
        out_specs=P(None, "gx", "gy"),
        check_vma=False,
    )
```

```python
import functools

import jax
import jax.numpy as jnp
from jax import lax
from jax.experimental import pallas as pl
from jax.experimental.pallas import tpu as pltpu
from jax.sharding import PartitionSpec as P

MESH = pl.DeviceIdType.MESH
NV = 14
NR = 8
PX = 12
CAP = 15
NZ = 32
GAS_GAMMA = 1.4
TIME_STEP = 0.025

ORIGIN = 16
OWN = ORIGIN * NV
NEXT = OWN + PX * NV
Y_ORIGIN = 12
Y_OWN = Y_ORIGIN * NV
Y_NEXT = Y_OWN + PX * NV
V_OWN = 4 * NV
G_OWN = 12 * NV

PARTS = ((0, 42, 0), (0, 32, 128), (136, 8, 224))
RUN_PART = (96, 11, 248)
RUN = 32
ROW0 = 11

W_ROWS = 672
Y_ROWS = 544
V_ROWS = 56 + 24 * NV
G_ROWS = 352

LOW = (2.0, -13.0, 47.0, 27.0, -3.0, 0.0)
HIGH = (0.0, -3.0, 27.0, 47.0, -13.0, 2.0)


def stencil_pair(q):
    d = [c / 60.0 for c in (2.0, 13.0, 47.0, 27.0, 3.0)]
    low = (d[0] * q[0] - d[1] * q[1]) + (d[2] * q[2] + d[3] * q[3]) - d[4] * q[4]
    high = (d[3] * q[2] - d[4] * q[1]) + (d[2] * q[3] - d[1] * q[4]) + d[0] * q[5]
    return low, high


def wave_speed(normal, pressure, density):
    scaled = GAS_GAMMA * pressure
    return jnp.abs(normal) + jnp.abs(scaled) * lax.rsqrt(jnp.maximum(scaled * density, 1e-30))


def face_flux(low, high, direction):
    rho_l, rho_r, p_l, p_r = low(0), high(0), low(4), high(4)
    u_l = [low(1 + j) for j in range(3)]
    u_r = [high(1 + j) for j in range(3)]
    n_l, n_r = u_l[direction], u_r[direction]
    speed = jnp.maximum(wave_speed(n_l, p_l, rho_l), wave_speed(n_r, p_r, rho_r))
    a_l, a_r = 0.5 * (n_l + speed), 0.5 * (n_r - speed)
    m_l, m_r = rho_l * a_l, rho_r * a_r
    flux = [m_l + m_r]
    for j in range(3):
        f = m_l * u_l[j] + m_r * u_r[j]
        if j == direction:
            f = f + 0.5 * (p_l + p_r)
        flux.append(f)
    k_l = u_l[0] * u_l[0] + u_l[1] * u_l[1] + u_l[2] * u_l[2]
    k_r = u_r[0] * u_r[0] + u_r[1] * u_r[1] + u_r[2] * u_r[2]
    flux.append(
        p_l * (2.5 * a_l + 0.5 * n_l) + p_r * (2.5 * a_r + 0.5 * n_r) + 0.5 * (m_l * k_l + m_r * k_r)
    )
    for j in range(5, NV):
        flux.append(m_l * low(j) + m_r * high(j))
    return flux


def primitives(c):
    inverse = 1.0 / c[0]
    u = [c[j] * inverse for j in (1, 2, 3)]
    kinetic = 0.5 * (c[1] * u[0] + c[2] * u[1] + c[3] * u[2])
    return [c[0]] + u + [0.4 * (c[4] - kinetic)] + [c[j] * inverse for j in range(5, NV)]


def lane():
    return lax.broadcasted_iota(jnp.int32, (8, 128), 1)


def fill_weights(weights):
    a = lax.broadcasted_iota(jnp.int32, (128, 128), 0)
    b = lax.broadcasted_iota(jnp.int32, (128, 128), 1)
    ga, gb, za, zb = a // NZ, b // NZ, a % NZ, b % NZ
    for slot in range(4):
        if slot == 3:
            offset = jnp.where(ga == gb, (za - zb + 3 + NZ) % NZ, NZ)
        else:
            offset = jnp.where(za == zb, 4 * (slot - 1) + ga - gb + 3, NZ)
        for side, coefficients in enumerate((LOW, HIGH)):
            w = jnp.zeros((128, 128), jnp.float32)
            for m, c in enumerate(coefficients):
                if c:
                    w = jnp.where(offset == m, c, w)
            w = w.astype(jnp.bfloat16)
            weights[slot, 0:128, 128 * side : 128 * side + 128] = w
            weights[slot, 128:256, 128 * side : 128 * side + 128] = w


def split_tile(q, qb, t, row, blocks):
    size = 8 * blocks
    x = q[:, t, row : row + size, :].reshape(NV * size, 128) * (1.0 / 60.0)
    top = x.astype(jnp.bfloat16)
    qb[t, 0 : NV * size, 0:128] = top
    qb[t, 0 : NV * size, 128:256] = (x - top.astype(jnp.float32)).astype(jnp.bfloat16)


def dot(a, b):
    return jnp.dot(a, b, preferred_element_type=jnp.float32)


def store_primitives(q, t, row, c):
    for v, value in enumerate(primitives(c)):
        q[v, t, row : row + 8, :] = value


def inner_terms(q, qb, fs, fx, s, weights, rate, row=ROW0, blocks=2):
    pre, act, heat = rate
    size = 8 * blocks
    for t in (1, 2):
        split_tile(q, qb, t, row, blocks)
    x, y = qb[1, 0 : NV * size], qb[2, 0 : NV * size]
    fs[0, 0 : NV * size] = dot(x, weights[3])
    fs[1, 0 : NV * size] = dot(y, weights[3])
    fs[2, 0 : NV * size] = dot(x, weights[1]) + dot(y, weights[2])
    fs[3, 0 : NV * size] = dot(x, weights[0]) + dot(y, weights[1])
    fs[4, 0 : NV * size] = dot(y, weights[0])
    first = lane() % NZ == NZ - 1

    def half(h, _):
        for kt in range(2):
            stencil = [
                [q[v, h + 1, row - 3 + 8 * kt + m : row + 5 + 8 * kt + m, :] for m in range(6)] for v in range(NV)
            ]
            pairs = [stencil_pair(x) for x in stencil]
            for v, f in enumerate(face_flux(lambda v: pairs[v][0], lambda v: pairs[v][1], 0)):
                fx[v, h, 8 * kt : 8 * kt + 8, :] = f
        for kt in range(blocks):
            rows = slice(8 * kt, 8 * kt + 8)
            cells = slice(row + 8 * kt, row + 8 * kt + 8)
            rho, pressure = q[0, h + 1, cells, :], q[4, h + 1, cells, :]
            ratio = rho / pressure
            rates = [
                pre[r] * rho * q[5 + r, h + 1, cells, :] * jnp.exp(-act[r] * ratio) for r in range(NR)
            ]
            release = heat[0] * rates[0]
            for r in range(1, NR):
                release = release + heat[r] * rates[r]
            source = [None] * 4 + [release, -rates[0]]
            source += [rates[r - 1] - rates[r] for r in range(1, NR)] + [rates[NR - 1]]
            flux = face_flux(
                lambda v: fs[h, size * v + 8 * kt : size * v + 8 * kt + 8, 0:128],
                lambda v: fs[h, size * v + 8 * kt : size * v + 8 * kt + 8, 128:256],
                2,
            )
            for v, f in enumerate(flux):
                above = jnp.where(first, pltpu.roll(f, NZ - 1, 1), pltpu.roll(f, 127, 1))
                x = (f - above) + (fx[v, h, rows, :] - fx[v, h, 8 * kt + 1 : 8 * kt + 9, :])
                if source[v] is not None:
                    x = x + source[v]
                s[v, h, rows, :] = x
        return 0

    lax.fori_loop(0, 2, half, 0)


def row_terms(q, qb, fs, fy, weights, row=ROW0, blocks=2):
    size = 8 * blocks
    split_tile(q, qb, 0, row, blocks)
    split_tile(q, qb, 3, row, blocks)
    x, y = qb[0, 0 : NV * size], qb[3, 0 : NV * size]
    fs[2, 0 : NV * size] += dot(x, weights[0])
    fs[3, 0 : NV * size] += dot(y, weights[2])
    fs[4, 0 : NV * size] += dot(y, weights[1])

    def tile(j, _):
        for kt in range(blocks):
            flux = face_flux(
                lambda v: fs[j + 2, size * v + 8 * kt : size * v + 8 * kt + 8, 0:128],
                lambda v: fs[j + 2, size * v + 8 * kt : size * v + 8 * kt + 8, 128:256],
                1,
            )
            for v, f in enumerate(flux):
                fy[v, j, 8 * kt : 8 * kt + 8, :] = f
        return 0

    lax.fori_loop(0, 3, tile, 0)


def rate_of(s, fy, v, h, kt):
    rows = slice(8 * kt, 8 * kt + 8)
    f = fy[v, h, rows, :]
    last = lane() >= 96
    above = jnp.where(last, pltpu.roll(fy[v, h + 1, rows, :], 96, 1), pltpu.roll(f, 96, 1))
    return s[v, h, rows, :] + (f - above)


def mirrored(x, sign):
    group = lane() // NZ
    return sign * jnp.where(group % 2 == 0, pltpu.roll(x, 32, 1), pltpu.roll(x, 96, 1))


def pack(src, start, quarter, dst, to, free):
    group = lax.broadcasted_iota(jnp.int32, (quarter, 128), 1) // NZ
    last = src(start + 3 * quarter, quarter)
    for j in range(3):
        moved = pltpu.roll(last, (32 * (3 - j) if free == 3 else 128 - 32 * (j + 1)), 1)
        dst[to + j * quarter : to + (j + 1) * quarter, :] = jnp.where(
            group == free, moved, src(start + j * quarter, quarter)
        )


def unpack(src, start, quarter, dst, to, free):
    group = lax.broadcasted_iota(jnp.int32, (quarter, 128), 1) // NZ
    last = jnp.ones((quarter, 128), jnp.float32)
    for j in range(3):
        x = src[start + j * quarter : start + (j + 1) * quarter, :]
        dst[to + j * quarter : to + (j + 1) * quarter, :] = jnp.where(group == free, 1.0, x)
        last = jnp.where(group == (j if free == 3 else j + 1), pltpu.roll(x, 32 * (j + 1), 1), last)
    dst[to + 3 * quarter : to + 4 * quarter, :] = last


def kernel(n_gx, n_gy, u, fresh_in, slide, cuts_in, pre_in, act_in, heat_in, out, us, fresh, cuts, pre, act, heat, xw, yl, yh, fb, yf, xe, vw, xs, xl, xg, yl2, yh2, ps, yp, ps2, yp2,
           q, qb, fs, fx, fy, s, weights, send_sem, recv_sem, load_sem, late_sem):
    gx, gy = lax.axis_index("gx"), lax.axis_index("gy")
    has_prev, has_next = gx > 0, gx < n_gx - 1
    starts_run = jnp.logical_and(has_prev, lax.rem(gx, RUN) == 0)
    ends_run = jnp.logical_and(has_next, lax.rem(gx, RUN) == RUN - 1)
    has_below, has_above = gy > 0, gy < n_gy - 1
    inside = {-1: has_prev, 1: has_next}
    beside = {-1: has_below, 1: has_above}
    pairs = ((u, us), (fresh_in, fresh), (cuts_in, cuts), (pre_in, pre), (act_in, act), (heat_in, heat))
    loads = [pltpu.make_async_copy(a, b, load_sem.at[k]) for k, (a, b) in enumerate(pairs)]

    def both(a, b):
        return jnp.logical_and(a, b)

    goes_on, went_on = both(has_next, jnp.logical_not(ends_run)), both(has_prev, jnp.logical_not(starts_run))
    neighbours = [(a, b) for a in (-1, 0, 1) for b in (-1, 0, 1) if a or b]
    barrier = pltpu.get_barrier_semaphore()
    for dx, dy in neighbours:
        there = goes_on if dx == 1 else has_prev
        if dx and dy:
            there = both(there, beside[dy])
        elif dy:
            there = beside[dy]

        @pl.when(there)
        def _(dx=dx, dy=dy):
            pl.semaphore_signal(barrier, inc=1, device_id=(gx + dx, gy + dy), device_id_type=MESH)

    for load in loads:
        load.start()
    loads[0].wait()
    for p in range(PX):
        for h in range(2):
            xw[h, OWN + NV * p : OWN + NV * (p + 1), :] = us[p, :, 128 * h : 128 * h + 128]
    along = 1 + jnp.where(went_on, 1, 0) + jnp.where(has_next, 1, 0)
    across = 1 + jnp.where(has_below, 1, 0) + jnp.where(has_above, 1, 0)
    pl.semaphore_wait(barrier, along * across - 1)
    for dy in (-1, 0, 1):

        @pl.when(both(ends_run, beside[dy]) if dy else ends_run)
        def _(dy=dy):
            pl.semaphore_signal(late_sem, inc=1, device_id=(gx + 1, gy + dy), device_id_type=MESH)


    def remote(k, src, dst, dx, dy):
        return pltpu.make_async_remote_copy(
            src_ref=src, dst_ref=dst, send_sem=send_sem.at[k], recv_sem=recv_sem.at[k],
            device_id=(gx + dx, gy + dy), device_id_type=MESH,
        )

    x_first = [
        (has_next, remote(1, xw.at[:, OWN + 96 : NEXT], xw.at[:, OWN - 72 : OWN], 1, 0), has_prev),
    ]
    x_back = [(has_prev, remote(0, xw.at[:, OWN:NEXT], xw.at[:, NEXT : NEXT + PX * NV], -1, 0), has_next)]
    y_first, y_back, y_near = [], [], []
    lower = [(ends_run, remote(18, xw.at[:, OWN + 56 : OWN + 96], xe, 1, 0), starts_run)]
    for k, dy in enumerate((1, -1)):
        to, of = beside[dy], beside[-dy]
        for number, (go, come, dx, a, b) in enumerate((
            (ends_run, starts_run, 1, 248, 288),
            (has_prev, has_next, -1, 128, 224),
            (has_next, has_prev, 1, 224, 248),
        )):
            copy = remote(2 + 5 * k + number, ps.at[k, a:b], yp.at[k, a:b], dx, dy)
            (lower if a == 248 else y_back if dx < 0 else y_near).append((both(to, go), copy, both(of, come)))
        y_first.append((to, remote(5 + 5 * k, ps.at[k, 0:128], yp.at[k, 0:128], 0, dy), of))
        y_first.append((
            both(to, jnp.logical_not(has_next)),
            remote(6 + 5 * k, fb.at[1 - k], yf.at[k], 0, dy),
            both(of, jnp.logical_not(has_next)),
        ))

    def start(copies, now=True):
        for to, copy, _ in copies:

            @pl.when(both(to, now))
            def _(copy=copy):
                copy.start()

    def arrive(copies):
        for _, copy, of in copies:

            @pl.when(of)
            def _(copy=copy):
                copy.wait_recv()

    def leave(copies):
        for to, copy, _ in copies:

            @pl.when(to)
            def _(copy=copy):
                copy.wait_send()

    def pack_part(part):
        row, quarter, to = part
        for k, h in ((0, 1), (1, 0)):
            pack(lambda a, n, h=h: xw[h, a : a + n, :], OWN + row, quarter, ps.at[k], to, 3 * k)

    start(x_first)
    pack_part(PARTS[2])
    start(y_near)
    start(lower[:1])

    @pl.when(ends_run)
    def _():
        pack_part(RUN_PART)

    start(lower[1:])
    pack_part(PARTS[1])
    start(y_back, went_on)
    pack_part(PARTS[0])
    for load in loads[1:]:
        load.wait()
    for h in range(2):
        fb[h, 0:NV, :] = fresh[:, 128 * h : 128 * h + 128]
        fb[h, NV:16, :] = jnp.zeros((2, 128), jnp.float32)
    start(y_first)
    start(x_back, went_on)
    base = jnp.clip(cuts[gx] - gx * PX + slide[0], -2, 9)
    count = jnp.clip(cuts[gx + 1] - cuts[gx], 9, CAP)
    fill_weights(weights)
    row_id = lax.broadcasted_iota(jnp.int32, (8, 128), 0)

    @pl.when(starts_run)
    def _():
        pl.semaphore_wait(late_sem, across)

    start(x_back, starts_run)
    start(y_back, starts_run)
    arrive(x_back)
    arrive(x_first)

    @pl.when(jnp.logical_not(has_next))
    def _():
        for p in range(12, 27):
            for h in range(2):
                xw[h, OWN + NV * p : OWN + NV * (p + 1), :] = fb[h, 0:NV, :]

    def window(h, k, v):
        return xw[h, pl.ds((base + ORIGIN + k) * NV + v, 8, stride=NV), :]

    low_edge = both(jnp.logical_not(has_prev), row_id < 3)

    def window_tile(h, _):
        for j in range(3):
            c = [window(h, 8 * j - 3, v) for v in range(NV)]
            if j == 0:
                c = [jnp.where(low_edge, xw[h, pl.ds((base + ORIGIN) * NV + v, 1), :], c[v]) for v in range(NV)]
            store_primitives(q, h + 1, 8 * j + 8, c)
        return 0

    lax.fori_loop(0, 2, window_tile, 0)
    inner_terms(q, qb, fs, fx, s, weights, (pre, act, heat))

    arrive(y_back)
    arrive(y_near)
    arrive(y_first)
    for k, ghost in ((0, yl), (1, yh)):
        for (_, quarter, row), to in zip(PARTS, (Y_OWN, Y_NEXT, Y_OWN - 32)):
            unpack(yp.at[k], row, quarter, ghost, to, 3 * k)

    @pl.when(jnp.logical_not(has_next))
    def _():
        for p in range(12, 21):
            for ghost, k in ((yl, 0), (yh, 1)):
                ghost[Y_OWN + NV * p : Y_OWN + NV * (p + 1), :] = yf[k, 0:NV, :]

    def beside_tiles(k):
        for t, h, ghost, is_wall in ((0, 0, yl, jnp.logical_not(has_below)), (3, 1, yh, jnp.logical_not(has_above))):

            @pl.when(is_wall)
            def _(t=t, h=h):
                c = [mirrored(window(h, k, v), -1.0 if v == 2 else 1.0) for v in range(NV)]
                store_primitives(q, t, ROW0 + k, c)

            @pl.when(jnp.logical_not(is_wall))
            def _(t=t, ghost=ghost):
                c = [ghost[pl.ds((base + Y_ORIGIN + k) * NV + v, 8, stride=NV), :] for v in range(NV)]
                store_primitives(q, t, ROW0 + k, c)

    for k in (0, 8):
        beside_tiles(k)

    row_terms(q, qb, fs, fy, weights)

    y_second = [
        (has_above, remote(14, ps2.at[0], yp2.at[0], 0, 1), has_below),
        (has_below, remote(15, ps2.at[1], yp2.at[1], 0, -1), has_above),
    ]
    for k, h in ((0, 1), (1, 0)):
        for kt in range(2):
            for v in range(NV):
                x = window(h, 8 * kt, v) + TIME_STEP * rate_of(s, fy, v, h, kt)
                vw[h, pl.ds(V_OWN + 8 * kt * NV + v, 8, stride=NV), :] = x
        pack(lambda a, n, h=h: vw[h, a : a + n, :], V_OWN, 56, ps2.at[k], 0, 3 * k)
        start(y_second[k : k + 1])
    for h in range(2):
        xs[h] = vw[h, pl.ds(V_OWN + (count - 3) * NV - 6, 48), :]
    second = [
        (has_prev, remote(12, vw.at[:, V_OWN : V_OWN + 48], xg.at[:, G_OWN : G_OWN + 48], -1, 0), has_next),
        (goes_on, remote(13, xs, xl.at[:, 0:48], 1, 0), went_on),
    ]
    start(second)

    @pl.when(jnp.logical_not(has_next))
    def _():
        for p in range(3):
            for h in range(2):
                xg[h, G_OWN + NV * p : G_OWN + NV * (p + 1), :] = fb[h, 0:NV, :]

    arrive(lower)

    @pl.when(starts_run)
    def _():
        for h in range(2):
            xw[h, OWN - 112 : OWN - 72, :] = xe[h]
        for k, ghost in ((0, yl), (1, yh)):
            unpack(yp.at[k], RUN_PART[2], RUN_PART[1], ghost, Y_OWN - 72, 3 * k)

        def lower_tile(h, _):
            store_primitives(q, h + 1, 0, [window(h, -ROW0, v) for v in range(NV)])
            return 0

        lax.fori_loop(0, 2, lower_tile, 0)
        beside_tiles(-8)
        inner_terms(q, qb, fs, fx, s, weights, (pre, act, heat), ROW0 - 8, 1)
        row_terms(q, qb, fs, fy, weights, ROW0 - 8, 1)

        def lower_update(h, _):
            for v in range(NV):
                x = window(h, -8, v) + TIME_STEP * rate_of(s, fy, v, h, 0)
                xl[h, pl.ds(6 + v, 3, stride=NV), :] = x[5:8]
            return 0

        lax.fori_loop(0, 2, lower_update, 0)

    arrive(second)

    def second_tile(h, _):
        for j in range(3):
            k = 8 * j - 3
            c = [vw[h, pl.ds(V_OWN + k * NV + v, 8, stride=NV), :] for v in range(NV)]
            if j == 0:
                ghosts = [xl[h, pl.ds(6 + v, 8, stride=NV), :] for v in range(NV)]
                c = [jnp.where(row_id < 3, ghosts[v], c[v]) for v in range(NV)]
                c = [jnp.where(low_edge, vw[h, V_OWN + v : V_OWN + v + 1, :], c[v]) for v in range(NV)]
            else:
                owned = row_id + k < count
                c = [
                    jnp.where(owned, c[v], xg[h, pl.ds(G_OWN + (k - count) * NV + v, 8, stride=NV), :])
                    for v in range(NV)
                ]
            store_primitives(q, h + 1, 8 * j + 8, c)
        return 0

    lax.fori_loop(0, 2, second_tile, 0)
    inner_terms(q, qb, fs, fx, s, weights, (pre, act, heat))

    arrive(y_second)
    for k, ghost in ((0, yl2), (1, yh2)):
        unpack(yp2.at[k], 0, 56, ghost, 0, 3 * k)
    for t, h, ghost, is_wall in ((0, 0, yl2, jnp.logical_not(has_below)), (3, 1, yh2, jnp.logical_not(has_above))):
        for kt in range(2):

            @pl.when(is_wall)
            def _(t=t, h=h, kt=kt):
                c = [
                    mirrored(vw[h, pl.ds(V_OWN + 8 * kt * NV + v, 8, stride=NV), :], -1.0 if v == 2 else 1.0)
                    for v in range(NV)
                ]
                store_primitives(q, t, ROW0 + 8 * kt, c)

            @pl.when(jnp.logical_not(is_wall))
            def _(t=t, ghost=ghost, kt=kt):
                c = [ghost[pl.ds(8 * kt * NV + v, 8, stride=NV), :] for v in range(NV)]
                store_primitives(q, t, ROW0 + 8 * kt, c)

    row_terms(q, qb, fs, fy, weights)
    for h in range(2):
        for kt in range(2):
            owned = row_id + 8 * kt < count
            for v in range(NV):
                w = window(h, 8 * kt, v)
                x = vw[h, pl.ds(V_OWN + 8 * kt * NV + v, 8, stride=NV), :] + TIME_STEP * rate_of(s, fy, v, h, kt)
                x = jnp.where(owned, 0.75 * w + 0.25 * x, 0.0)
                if kt == 0:
                    out[v, 0:8, 128 * h : 128 * h + 128] = x
                else:
                    out[v, 8:CAP, 128 * h : 128 * h + 128] = x[0 : CAP - 8]

    leave(lower)
    leave(x_back)
    leave(y_back)
    leave(x_first)
    leave(y_near)
    leave(y_first)
    leave(second)
    leave(y_second)


def body(n_gx, n_gy, gas_state, inflow, slide_count, cut_list, prefactor, activation, heat_release):
    def f32(*shape):
        return pltpu.VMEM(shape, jnp.float32)

    return pl.pallas_call(
        functools.partial(kernel, n_gx, n_gy),
        out_shape=pltpu.VMEM((NV, CAP, 256), jnp.float32),
        in_specs=[pl.BlockSpec(memory_space=m) for m in [pltpu.HBM] * 2 + [pltpu.SMEM] + [pltpu.HBM] * 4],
        out_specs=pl.BlockSpec(memory_space=pltpu.VMEM),
        scratch_shapes=[
            f32(PX, NV, 256),
            f32(NV, 256),
            pltpu.SMEM((n_gx + 1,), jnp.int32),
            pltpu.SMEM((NR,), jnp.float32),
            pltpu.SMEM((NR,), jnp.float32),
            pltpu.SMEM((NR,), jnp.float32),
            f32(2, W_ROWS, 128),
            f32(Y_ROWS, 128),
            f32(Y_ROWS, 128),
            f32(2, 16, 128),
            f32(2, 16, 128),
            f32(2, 40, 128),
            f32(2, V_ROWS, 128),
            f32(2, 48, 128),
            f32(2, 136, 128),
            f32(2, G_ROWS, 128),
            f32(240, 128),
            f32(240, 128),
            f32(2, 288, 128),
            f32(2, 288, 128),
            f32(2, 168, 128),
            f32(2, 168, 128),
            f32(NV, 4, 32, 128),
            pltpu.VMEM((4, NV * 16, 256), jnp.bfloat16),
            f32(5, NV * 16, 256),
            f32(NV, 2, 24, 128),
            f32(NV, 3, 16, 128),
            f32(NV, 2, 16, 128),
            pltpu.VMEM((4, 256, 256), jnp.bfloat16),
            pltpu.SemaphoreType.DMA((19,)),
            pltpu.SemaphoreType.DMA((19,)),
            pltpu.SemaphoreType.DMA((6,)),
            pltpu.SemaphoreType.REGULAR,
        ],
        compiler_params=pltpu.CompilerParams(
            collective_id=0, has_side_effects=True, vmem_limit_bytes=32 * 1024 * 1024
        ),
        name="two_stages",
    )(*[
        x if x is slide_count else pltpu.with_memory_space_constraint(x, pltpu.HBM)
        for x in (
            jnp.transpose(gas_state, (1, 0, 2)), inflow, slide_count, cut_list, prefactor, activation, heat_release
        )
    ])


def solution(mesh):
    in_specs = (P(None, "gx", "gy"), P(None, "gy"), P(), P(), P(), P(), P())
    return jax.shard_map(
        functools.partial(body, mesh.shape["gx"], mesh.shape["gy"]),
        mesh=mesh,
        in_specs=in_specs,
        out_specs=P(None, "gx", "gy"),
        check_vma=False,
    )
```
